32 devices in a mesh: groups: 2 (over x), seq: 16 (over z, y, core).
Axes of the slice: x: 2, y: 2, z: 4, core: 2. Of those that a mesh axis runs over, the one named last changes fastest.
Arguments:
- tokens: bfloat16 [4096, 1536], P(('groups', 'seq')), parts along dimension 0, may hold values from -6 to 6
- control: bfloat16 [4096, 1536], P(('groups', 'seq')), parts along dimension 0, may hold values from -1800 to 1800, as said below
- zero_weight: bfloat16 [1536, 1536], P(None, 'seq'), may hold values from -0.15625 to 0.15625
- modulation: float32 [6, 1536], P('groups'), parts along dimension 0, may hold values from -1 to 1.5, as said below
- qkv_weight: bfloat16 [1536, 2304], replicated, may hold values from -0.15625 to 0.15625
- out_weight: bfloat16 [768, 1536], replicated, may hold values from -0.21875 to 0.21875
Outputs:
- block_out: bfloat16 [4096, 1536], P(('groups', 'seq')), parts along dimension 0
The draws below stay inside these ranges and needn't reach their ends.
There are 2 independent parts, one for each index of `groups`. The reference program is written for one: setup_inputs(seed, part) draws one part's arguments, and reference() takes and returns one part's arrays. A program takes and returns all parts, laid end to end along the dimension named above; an argument that names none is the same for every part. Nothing has to cross between parts.
Inputs may be any that keep to these rules, and one draw needn't show every extreme that they name: Features of the control block, of varied scales. `modulation`: row 0 shifts, row 1 scales, row 2 gates.
All inputs are finite; a program needn't handle non-finite values.
Results may differ from the reference program's by a relative error of at most 0.025.
Values may be sent and summed in bfloat16 or wider, within the bound.
A program may use at most 192 MiB of HBM per device.

```python
import math
import jax
import jax.numpy as jnp
from jax import lax

D = 1536
HEADS = 12
HEAD = 64
GROUPS = 32
VIEWS = 8
TOKENS = 2048
VIEW_TOK = 256
HH = 768


def draw_control(key, part):
    key = jax.random.fold_in(key, 11)
    first, second, third = jax.random.split(key, 3)
    rising = 3.0 ** (jnp.arange(TOKENS, dtype=jnp.float32) / TOKENS)
    row_scale = 10.0 ** jax.random.uniform(first, (TOKENS, 1), jnp.float32) * rising[:, None]
    col_scale = 10.0 ** jax.random.uniform(second, (1, D), jnp.float32)
    base = jnp.clip(jax.random.normal(third, (TOKENS, D), jnp.float32), -6.0, 6.0)
    return (base * row_scale * col_scale).astype(jnp.bfloat16)


def draw_modulation(key, part):
    key = jax.random.fold_in(key, 12)
    first, second, third = jax.random.split(key, 3)
    shifts = jax.random.uniform(first, (D,), jnp.float32, -0.8, 0.8)
    scales = jax.random.uniform(second, (D,), jnp.float32, -0.5, 1.5)
    gates = jax.random.uniform(third, (D,), jnp.float32, 0.5, 1.5)
    return jnp.stack([shifts, scales, gates]).astype(jnp.float32)


def block_levels(own_key, dims, cuts, least, top_value):
    loudness = 1.0
    for axis_at, shards_of in cuts:
        draws = jax.random.uniform(jax.random.fold_in(jax.random.fold_in(own_key, 6), axis_at), (shards_of,), jnp.float32, least / len(cuts), top_value / len(cuts))
        loudness = loudness * jnp.repeat(jnp.exp(draws), dims[axis_at] // shards_of).reshape((-1,) + (1,) * (len(dims) - 1 - axis_at))
    return loudness


def scatter_about(key, dims, scale, limit, cuts=(), kind=jnp.bfloat16):
    array = scale * jax.random.normal(key, dims, jnp.float32)
    if cuts:
        array = array * block_levels(key, dims, cuts, -0.22, 0.18)
    return jnp.clip(array, -limit, limit).astype(kind)


def setup_inputs(seed: int = 0, part: int = 0) -> dict:
    splits = jax.random.split(jax.random.key(seed), 7)
    part_splits = jax.random.split(jax.random.fold_in(splits[6], part), 7)
    tokens = scatter_about(part_splits[0], (TOKENS, D), 1.0, 6.0, ((0, 16),))
    control = draw_control(jax.random.fold_in(jax.random.fold_in(splits[6], part), 71), part)
    zero_weight = scatter_about(splits[2], (D, D), D ** -0.5, 0.15625, ((1, 16),))
    modulation = draw_modulation(jax.random.fold_in(jax.random.fold_in(splits[6], part), 71), part)
    qkv_weight = scatter_about(splits[4], (D, 3 * HH), D ** -0.5, 0.15625)
    out_weight = scatter_about(splits[5], (HH, D), HH ** -0.5, 0.21875)
    return {"tokens": tokens, "control": control, "zero_weight": zero_weight, "modulation": modulation, "qkv_weight": qkv_weight, "out_weight": out_weight}


def reference(tokens, control, zero_weight, modulation, qkv_weight, out_weight):
    per_group = D // GROUPS
    control_f = control.astype(jnp.float32).reshape(VIEWS, VIEW_TOK, GROUPS, per_group)
    count = VIEW_TOK * per_group
    view_mean = lax.optimization_barrier(jnp.sum(control_f, axis=(1, 3), keepdims=True)) / count
    centered = control_f - view_mean
    view_var = lax.optimization_barrier(jnp.sum(centered * centered, axis=(1, 3), keepdims=True)) / count
    normed = (centered / jnp.sqrt(view_var + 1e-05)).reshape(TOKENS, D).astype(jnp.bfloat16)
    residual = jnp.dot(normed, zero_weight, preferred_element_type=jnp.float32)
    hidden = (tokens.astype(jnp.float32) + residual).astype(jnp.bfloat16)
    hidden_f = hidden.astype(jnp.float32)
    tok_mean = lax.optimization_barrier(jnp.mean(hidden_f, axis=-1, keepdims=True))
    tok_dev = hidden_f - tok_mean
    tok_var = lax.optimization_barrier(jnp.mean(tok_dev * tok_dev, axis=-1, keepdims=True))
    layered = tok_dev / jnp.sqrt(tok_var + 1e-06)
    adapted = (layered * (1.0 + modulation[1]) + modulation[0]).astype(jnp.bfloat16)
    projected = jnp.dot(adapted, qkv_weight, preferred_element_type=jnp.float32)
    query = projected[:, :HH].astype(jnp.bfloat16)
    key_all = projected[:, HH:2 * HH].astype(jnp.bfloat16).astype(jnp.float32).reshape(TOKENS, HEADS, HEAD)
    value_all = projected[:, 2 * HH:].astype(jnp.bfloat16).astype(jnp.float32).reshape(TOKENS, HEADS, HEAD)
    scale = 1.0 / math.sqrt(HEAD)
    block_len = math.gcd(TOKENS, 512)

    def attend(query_block):
        query_heads = query_block.astype(jnp.float32).reshape(block_len, HEADS, HEAD)
        scores = jnp.einsum('qhd,khd->hqk', query_heads, key_all) * scale
        rowmax = lax.optimization_barrier(jnp.max(scores, axis=-1, keepdims=True))
        expo = jnp.exp(scores - rowmax)
        total = lax.optimization_barrier(jnp.sum(expo, axis=-1))
        probs = lax.optimization_barrier(expo.astype(jnp.bfloat16)).astype(jnp.float32)
        mixed = jnp.einsum('hqk,khd->qhd', probs, value_all)
        mixed = mixed / jnp.transpose(total)[:, :, None]
        return mixed.reshape(block_len, HH).astype(jnp.bfloat16)
    attended = lax.map(attend, query.reshape(TOKENS // block_len, block_len, HH)).reshape(TOKENS, HH)
    projected_out = jnp.dot(attended, out_weight, preferred_element_type=jnp.float32)
    return (hidden_f + modulation[2] * projected_out).astype(jnp.bfloat16)
```

```python
import functools

import jax
import jax.numpy as jnp
from jax import lax
from jax.experimental import pallas as pl
from jax.experimental.pallas import tpu as pltpu
from jax.sharding import PartitionSpec as P

HEADS = 12
HEAD = 64
GROUPS = 32
VIEWS = 8
SPLIT = 4
LANES = 128
MESH = pl.DeviceIdType.MESH


def flip(index, d):
    if d == 0:
        return index
    if d == 1:
        return index + 1 - 2 * (index % 2)
    if d == 2:
        return index + 2 - 4 * (index // 2)
    return 3 - index


def kernel(
    n,
    gather,
    tokens_ref,
    control_ref,
    w_ref,
    mod_ref,
    qkv_hbm,
    out_hbm,
    result_ref,
    wbuf,
    qkv_w,
    out_w,
    stat,
    hidden,
    adapted,
    pack,
    qpack,
    kvb,
    qbuf,
    obuf,
    osend,
    m_ref,
    l_ref,
    acc_ref,
    load_sem,
    stat_s,
    stat_r,
    wz_s,
    wz_r,
    wy_s,
    wy_r,
    wx_s,
    wx_r,
    wc_s,
    wc_r,
    kz_s,
    kz_r,
    ky_s,
    ky_r,
    kc_s,
    kc_r,
    q_s,
    q_r,
    o_s,
    o_r,
):
    rows, width = tokens_ref.shape
    per_group = width // GROUPS
    cols = width // n
    members = n // SPLIT
    pairs = members // 2
    span = n // VIEWS
    me_g = lax.axis_index("groups")
    me = lax.axis_index("seq")
    hh = me // members
    uu = (me % members) // 2
    cc = me % 2

    def at(h, u, c):
        return (me_g, (h * pairs + u) * 2 + c)

    sibling = at(hh, uu, 1 - cc)
    zmate = [at(flip(hh, d), uu, cc) for d in range(SPLIT)]
    ymate = [at(hh, (uu + f) % pairs, cc) for f in range(pairs)]
    xmate = (1 - me_g, me)
    view_base = (me // span) * span
    peer = [(me_g, view_base + (me - view_base + f) % span) for f in range(span)]

    loads = [
        pltpu.make_async_copy(qkv_hbm, qkv_w, load_sem.at[0]),
        pltpu.make_async_copy(out_hbm, out_w, load_sem.at[1]),
    ]
    if not gather:
        loads.append(pltpu.make_async_copy(w_ref, wbuf, load_sem.at[2]))
    for load in loads:
        load.start()

    barrier = pltpu.get_barrier_semaphore()
    greet = [sibling] + zmate[1:] + ymate[1:] + peer[1:] + ([xmate] if gather else [])
    for device in greet:
        pl.semaphore_signal(barrier, inc=1, device_id=device, device_id_type=MESH)

    if gather:
        wbuf[pl.ds(pl.multiple_of(me * cols, cols), cols), :] = jnp.transpose(w_ref[...])

    pl.semaphore_wait(barrier, len(greet))

    sent = []

    def send(src, dst, ssem, rsem, device):
        copy = pltpu.make_async_remote_copy(
            src_ref=src, dst_ref=dst, send_sem=ssem, recv_sem=rsem, device_id=device, device_id_type=MESH
        )
        copy.start()
        sent.append(copy)

    def arrive(dst, ssem, rsem):
        pltpu.make_async_remote_copy(
            src_ref=dst, dst_ref=dst, send_sem=ssem, recv_sem=rsem, device_id=sibling, device_id_type=MESH
        ).wait_recv()

    third = cols // 3

    def slab(e, d, c, start, count):
        owner = (flip(hh, d) * pairs + (uu + e) % pairs) * 2 + c
        return wbuf.at[pl.ds(pl.multiple_of(owner * cols + start, third), count), :]

    plane = third * me_g
    over_x = 2 * third * me_g
    from_x = 2 * third * (1 - me_g)

    def relay_y(d):
        for f in range(1, pairs):
            part = slab(0, d, cc, plane, 2 * third)
            send(part, part, wy_s.at[f, d], wy_r.at[f, d], ymate[f])

    def relay_x(e, d):
        part = slab(e, d, cc, over_x, third)
        send(part, part, wx_s.at[e, d], wx_r.at[e, d], xmate)

    def relay_c(e, d):
        part = slab(e, d, cc, plane, 2 * third)
        send(part, part, wc_s.at[0, e, d], wc_r.at[0, e, d], sibling)

    if gather:
        own = slab(0, 0, cc, plane, 2 * third)
        for d in range(1, SPLIT):
            send(own, own, wz_s.at[d], wz_r.at[d], zmate[d])
        relay_y(0)
        whole = slab(0, 0, cc, 0, cols)
        send(whole, whole, wc_s.at[0, 0, 0], wc_r.at[0, 0, 0], sibling)

    lane_group = lax.broadcasted_iota(jnp.int32, (width, LANES), 1) * per_group
    channel = lax.broadcasted_iota(jnp.int32, (width, LANES), 0)
    member = ((channel >= lane_group) & (channel < lane_group + per_group)).astype(jnp.float32)

    def group_sum(line):
        return lax.dot_general(
            line,
            member,
            (((1,), (0,)), ((), ())),
            precision=lax.Precision.HIGHEST,
            preferred_element_type=jnp.float32,
        )

    def spread(line):
        return lax.dot_general(
            line,
            member,
            (((1,), (1,)), ((), ())),
            precision=lax.Precision.HIGHEST,
            preferred_element_type=jnp.float32,
        )

    local_count = float(rows * per_group)
    control_f = control_ref[...].astype(jnp.float32)
    col_sum = jnp.sum(control_f, axis=0, keepdims=True)
    local_mean = group_sum(jnp.broadcast_to(col_sum, (8, width))) / local_count
    off = control_f - spread(local_mean)[0:1, :]
    col_sq = jnp.sum(off * off, axis=0, keepdims=True)
    local_m2 = group_sum(jnp.broadcast_to(col_sq, (8, width)))
    stat[0, 0] = local_mean
    stat[0, 1] = local_m2
    for f in range(1, span):
        send(stat.at[0], stat.at[f], stat_s.at[f], stat_r.at[f], peer[f])
    for f in range(1, span):
        arrive(stat.at[f], stat_s.at[f], stat_r.at[f])
    mean = stat[0, 0]
    m2 = stat[0, 1]
    for f in range(1, span):
        mean = mean + stat[f, 0]
        m2 = m2 + stat[f, 1]
    mean = mean / span
    for f in range(span):
        gap = stat[f, 0] - mean
        m2 = m2 + local_count * (gap * gap)
    var = m2 / (local_count * span)
    inv = 1.0 / jnp.sqrt(var + 1e-05)
    normed = ((control_ref[...].astype(jnp.float32) - spread(mean)[0:1, :]) * spread(inv)[0:1, :]).astype(
        jnp.bfloat16
    )

    if gather:
        for d in range(1, SPLIT):
            arrive(slab(0, d, cc, plane, 2 * third), wz_s.at[d], wz_r.at[d])
            relay_y(d)
            relay_x(0, d)
            relay_c(0, d)
            for e in range(1, pairs):
                f = pairs - e
                arrive(slab(e, d - 1, cc, plane, 2 * third), wy_s.at[f, d - 1], wy_r.at[f, d - 1])
                relay_x(e, d - 1)
                relay_c(e, d - 1)
        for e in range(1, pairs):
            f = pairs - e
            d = SPLIT - 1
            arrive(slab(e, d, cc, plane, 2 * third), wy_s.at[f, d], wy_r.at[f, d])
            relay_x(e, d)
            relay_c(e, d)
        order = [(0, d) for d in range(1, SPLIT)] + [(e, d) for d in range(SPLIT) for e in range(1, pairs)]
        for e, d in order:
            part = slab(e, d, cc, from_x, third)
            arrive(part, wx_s.at[e, d], wx_r.at[e, d])
            send(part, part, wc_s.at[1, e, d], wc_r.at[1, e, d], sibling)
    else:
        loads[2].wait()

    block = width // SPLIT
    for d in range(SPLIT):
        if gather:
            for e in range(pairs):
                if (e, d) == (0, 0):
                    arrive(slab(0, 0, 1 - cc, 0, cols), wc_s.at[0, 0, 0], wc_r.at[0, 0, 0])
                else:
                    arrive(slab(e, d, 1 - cc, plane, 2 * third), wc_s.at[0, e, d], wc_r.at[0, e, d])
                    arrive(slab(e, d, 1 - cc, from_x, third), wc_s.at[1, e, d], wc_r.at[1, e, d])
        place = pl.ds(pl.multiple_of(flip(hh, d) * block, block), block)
        residual = lax.dot_general(
            normed, wbuf[place, :], (((1,), (1,)), ((), ())), preferred_element_type=jnp.float32
        )
        hidden[:, place] = (tokens_ref[:, place].astype(jnp.float32) + residual).astype(jnp.bfloat16)

    hidden_f = hidden[...].astype(jnp.float32)
    tok_mean = jnp.mean(hidden_f, axis=-1, keepdims=True)
    tok_dev = hidden_f - tok_mean
    tok_var = jnp.mean(tok_dev * tok_dev, axis=-1, keepdims=True)
    layered = tok_dev / jnp.sqrt(tok_var + 1e-06)
    adapted[...] = (layered * (1.0 + mod_ref[1:2, :]) + mod_ref[0:1, :]).astype(jnp.bfloat16)

    features = HEADS * HEAD
    left = lax.broadcasted_iota(jnp.int32, (rows, LANES), 1) < HEAD
    loads[0].wait()

    def project(at_col):
        return jnp.dot(
            adapted[...], qkv_w[:, at_col : at_col + features], preferred_element_type=jnp.float32
        )

    def tile(array, i):
        return array[:, i * LANES : (i + 1) * LANES]

    def lone(array, g):
        held = tile(array, SPLIT + g // 2)
        return held if g % 2 == 0 else pltpu.roll(held, HEAD, 1)

    def lone_right(array, g):
        held = tile(array, SPLIT + g // 2)
        return held if g % 2 == 1 else pltpu.roll(held, HEAD, 1)

    key = project(features)
    value = project(2 * features)
    for g in range(SPLIT):
        pack[g, :, 0:LANES] = tile(key, g).astype(jnp.bfloat16)
        pack[g, :, LANES : 2 * LANES] = jnp.where(left, lone(key, g), lone_right(value, g)).astype(jnp.bfloat16)
        pack[g, :, 2 * LANES : 3 * LANES] = tile(value, g).astype(jnp.bfloat16)

    def spot(e, d, par):
        first = ((d * pairs + e) * 2 + par) * rows
        return kvb.at[pl.ds(first, rows), :]

    for d in range(1, SPLIT):
        send(pack.at[flip(hh, d)], spot(0, d, 0), kz_s.at[d], kz_r.at[d], zmate[d])
    kvb[0:rows, :] = pack[hh]

    def relay_kv(d):
        for f in range(1, pairs):
            send(spot(0, d, 0), spot(pairs - f, d, 0), ky_s.at[f, d], ky_r.at[f, d], ymate[f])
        send(spot(0, d, 0), spot(0, d, 1), kc_s.at[0, d], kc_r.at[0, d], sibling)

    relay_kv(0)

    query = project(0) * (1.0 / HEAD**0.5)
    for g in range(SPLIT):
        qpack[g, :, 0:LANES] = tile(query, g).astype(jnp.bfloat16)
        qpack[g, :, LANES : 2 * LANES] = jnp.where(left, lone(query, g), 0.0).astype(jnp.bfloat16)
    for d in range(1, SPLIT):
        send(qpack.at[flip(hh, d)], qbuf.at[d], q_s.at[d], q_r.at[d], zmate[d])
    qbuf[0] = qpack[hh]

    m_ref[...] = jnp.full_like(m_ref, -1e30)
    l_ref[...] = jnp.zeros_like(l_ref)
    acc_ref[...] = jnp.zeros_like(acc_ref)

    for d in range(1, SPLIT):
        arrive(spot(0, d, 0), kz_s.at[d], kz_r.at[d])
        relay_kv(d)
    for d in range(SPLIT):
        for e in range(1, pairs):
            f = pairs - e
            arrive(spot(e, d, 0), ky_s.at[f, d], ky_r.at[f, d])
            send(spot(e, d, 0), spot(e, d, 1), kc_s.at[e, d], kc_r.at[e, d], sibling)
    for d in range(1, SPLIT):
        arrive(qbuf.at[d], q_s.at[d], q_r.at[d])

    keys = members * rows
    for d in range(SPLIT):
        for e in range(pairs):
            arrive(spot(e, d, 1), kc_s.at[e, d], kc_r.at[e, d])

        @pl.loop(0, SPLIT)
        def _(t):
            for h in range(3):
                if h < 2:
                    q = qbuf[t, :, 0:LANES]
                    q = jnp.where(left if h == 0 else ~left, q, jnp.zeros_like(q))
                else:
                    q = qbuf[t, :, LANES : 2 * LANES]
                kt, vt = (0, 2) if h < 2 else (1, 1)
                k = kvb[d * keys : (d + 1) * keys, kt * LANES : (kt + 1) * LANES]
                v = kvb[d * keys : (d + 1) * keys, vt * LANES : (vt + 1) * LANES]
                scores = lax.dot_general(
                    q, k, (((1,), (1,)), ((), ())), preferred_element_type=jnp.float32
                )
                best = m_ref[h, t]
                new_best = jnp.maximum(best, jnp.max(scores, axis=-1, keepdims=True))
                shrink = jnp.exp(best - new_best)
                expo = jnp.exp(scores - new_best[:, 0:1])
                part = expo[:, 0:LANES]
                for i in range(1, keys // LANES):
                    part = part + expo[:, i * LANES : (i + 1) * LANES]
                m_ref[h, t] = new_best
                l_ref[h, t] = l_ref[h, t] * shrink + part
                acc_ref[h, t] = acc_ref[h, t] * shrink + jnp.dot(
                    expo.astype(jnp.bfloat16), v, preferred_element_type=jnp.float32
                )

    for t in range(SPLIT):
        mixed = [acc_ref[h, t] / jnp.sum(l_ref[h, t], axis=-1, keepdims=True) for h in range(3)]
        osend[t, :, 0:LANES] = jnp.where(left, mixed[0], mixed[1]).astype(jnp.bfloat16)
        osend[t, :, LANES : 2 * LANES] = mixed[2].astype(jnp.bfloat16)
        if t > 0:
            send(osend.at[t], obuf.at[hh], o_s.at[t], o_r.at[t], zmate[t])
    obuf[hh] = osend[0]
    for d in range(1, SPLIT):
        arrive(obuf.at[flip(hh, d)], o_s.at[d], o_r.at[d])
    loads[1].wait()

    parts = [obuf[g, :, 0:LANES] for g in range(SPLIT)]
    for g in range(0, SPLIT, 2):
        first = pltpu.roll(obuf[g, :, LANES : 2 * LANES].astype(jnp.float32), HEAD, 1)
        second = obuf[g + 1, :, LANES : 2 * LANES].astype(jnp.float32)
        parts.append(jnp.where(left, first, second).astype(jnp.bfloat16))
    attended = jnp.concatenate(parts, axis=1)
    projected_out = jnp.dot(attended, out_w[...], preferred_element_type=jnp.float32)
    result_ref[...] = (hidden[...].astype(jnp.float32) + mod_ref[2:3, :] * projected_out).astype(jnp.bfloat16)

    for copy in sent:
        copy.wait_send()


def per_device(n, groups, tokens, control, zero_weight, modulation, qkv_weight, out_weight):
    rows, width = tokens.shape
    cols = zero_weight.shape[1]
    members = n // SPLIT
    pairs = members // 2
    span = n // VIEWS
    gather = groups == 2 and cols % 48 == 0
    weight = zero_weight
    if not gather:
        weight = lax.all_gather(jnp.transpose(zero_weight), "seq", axis=0, tiled=True)
    vmem = pl.BlockSpec(memory_space=pltpu.VMEM)
    anywhere = pl.BlockSpec(memory_space=pl.ANY)
    bf16, f32, dma = jnp.bfloat16, jnp.float32, pltpu.SemaphoreType.DMA
    features = HEADS * HEAD
    return pl.pallas_call(
        functools.partial(kernel, n, gather),
        out_shape=jax.ShapeDtypeStruct((rows, width), bf16),
        in_specs=[vmem, vmem, vmem if gather else anywhere, vmem, anywhere, anywhere],
        out_specs=vmem,
        scratch_shapes=[
            pltpu.VMEM((width, width), bf16),
            pltpu.VMEM(qkv_weight.shape, bf16),
            pltpu.VMEM(out_weight.shape, bf16),
            pltpu.VMEM((span, 2, 8, LANES), f32),
            pltpu.VMEM((rows, width), bf16),
            pltpu.VMEM((rows, width), bf16),
            pltpu.VMEM((SPLIT, rows, 3 * LANES), bf16),
            pltpu.VMEM((SPLIT, rows, 2 * LANES), bf16),
            pltpu.VMEM((n * rows, 3 * LANES), bf16),
            pltpu.VMEM((SPLIT, rows, 2 * LANES), bf16),
            pltpu.VMEM((SPLIT, rows, 2 * LANES), bf16),
            pltpu.VMEM((SPLIT, rows, 2 * LANES), bf16),
            pltpu.VMEM((3, SPLIT, rows, LANES), f32),
            pltpu.VMEM((3, SPLIT, rows, LANES), f32),
            pltpu.VMEM((3, SPLIT, rows, LANES), f32),
            dma((3,)),
            dma((span,)),
            dma((span,)),
            dma((SPLIT,)),
            dma((SPLIT,)),
            dma((pairs, SPLIT)),
            dma((pairs, SPLIT)),
            dma((pairs, SPLIT)),
            dma((pairs, SPLIT)),
            dma((2, pairs, SPLIT)),
            dma((2, pairs, SPLIT)),
            dma((SPLIT,)),
            dma((SPLIT,)),
            dma((pairs, SPLIT)),
            dma((pairs, SPLIT)),
            dma((pairs, SPLIT)),
            dma((pairs, SPLIT)),
            dma((SPLIT,)),
            dma((SPLIT,)),
            dma((SPLIT,)),
            dma((SPLIT,)),
        ],
        compiler_params=pltpu.CompilerParams(
            collective_id=0, has_side_effects=True, vmem_limit_bytes=56 * 1024 * 1024
        ),
    )(tokens, control, weight, modulation, qkv_weight, out_weight)


def solution(mesh):
    placed = (
        P(("groups", "seq"), None),
        P(("groups", "seq"), None),
        P(None, "seq"),
        P("groups", None),
        P(),
        P(),
    )
    return jax.shard_map(
        functools.partial(per_device, mesh.shape["seq"], mesh.shape["groups"]),
        mesh=mesh,
        in_specs=placed,
        out_specs=P(("groups", "seq"), None),
        check_vma=False,
    )
```

```python
import functools

import jax
import jax.numpy as jnp
from jax import lax
from jax.experimental import pallas as pl
from jax.experimental.pallas import tpu as pltpu
from jax.sharding import PartitionSpec as P

HEADS = 12
HEAD = 64
GROUPS = 32
VIEWS = 8
QUERY_TILE = 256
SPLIT = 4
LANES = 128
MESH = pl.DeviceIdType.MESH


def flip(index, d):
    if d == 0:
        return index
    if d == 1:
        return index + 1 - 2 * (index % 2)
    if d == 2:
        return index + 2 - 4 * (index // 2)
    return 3 - index


def kernel(
    n,
    gather,
    tokens_hbm,
    control_hbm,
    w_hbm,
    mod_ref,
    qkv_hbm,
    out_hbm,
    result_ref,
    tokens_ref,
    control_ref,
    wbuf,
    nbuf,
    rbuf,
    mine,
    theirs,
    qkv_w,
    out_w,
    stat,
    hidden,
    adapted,
    pack,
    qpack,
    kvb,
    qbuf,
    obuf,
    osend,
    m_ref,
    l_ref,
    acc_ref,
    load_sem,
    stat_s,
    stat_r,
    wz_s,
    wz_r,
    ny_s,
    ny_r,
    ry_s,
    ry_r,
    wx_s,
    wx_r,
    wc_s,
    wc_r,
    kz_s,
    kz_r,
    ky_s,
    ky_r,
    kc_s,
    kc_r,
    q_s,
    q_r,
    o_s,
    o_r,
):
    rows, width = tokens_hbm.shape
    per_group = width // GROUPS
    cols = width // n
    members = n // SPLIT
    pairs = members // 2
    span = n // VIEWS
    me_g = lax.axis_index("groups")
    me = lax.axis_index("seq")
    hh = me // members
    uu = (me % members) // 2
    cc = me % 2

    def at(h, u, c):
        return (me_g, (h * pairs + u) * 2 + c)

    sibling = at(hh, uu, 1 - cc)
    zmate = [at(flip(hh, d), uu, cc) for d in range(SPLIT)]
    ymate = [at(hh, (uu + f) % pairs, cc) for f in range(pairs)]
    xmate = (1 - me_g, me)
    view_base = (me // span) * span
    peer = [(me_g, view_base + (me - view_base + f) % span) for f in range(span)]

    loads = [
        pltpu.make_async_copy(qkv_hbm, qkv_w, load_sem.at[0]),
        pltpu.make_async_copy(out_hbm, out_w, load_sem.at[1]),
        pltpu.make_async_copy(control_hbm, control_ref, load_sem.at[2]),
        pltpu.make_async_copy(tokens_hbm, tokens_ref, load_sem.at[3]),
    ]
    loads = [loads[2], loads[3], loads[0], loads[1]]
    load_control, load_tokens, load_qkv, load_out = loads
    if gather:
        place = pl.ds(pl.multiple_of((hh * 2 + cc) * cols, cols), cols)
        load_w = pltpu.make_async_copy(w_hbm, wbuf.at[place, :], load_sem.at[4])
    else:
        load_w = pltpu.make_async_copy(w_hbm, wbuf, load_sem.at[4])
    loads.append(load_w)
    for load in loads:
        load.start()

    barrier = pltpu.get_barrier_semaphore()
    greet = [sibling] + zmate[1:] + ymate[1:] + peer[1:] + ([xmate] if gather else [])
    for device in greet:
        pl.semaphore_signal(barrier, inc=1, device_id=device, device_id_type=MESH)

    pl.semaphore_wait(barrier, len(greet))

    sent = []

    def send(src, dst, ssem, rsem, device):
        copy = pltpu.make_async_remote_copy(
            src_ref=src, dst_ref=dst, send_sem=ssem, recv_sem=rsem, device_id=device, device_id_type=MESH
        )
        copy.start()
        sent.append(copy)

    def arrive(dst, ssem, rsem):
        pltpu.make_async_remote_copy(
            src_ref=dst, dst_ref=dst, send_sem=ssem, recv_sem=rsem, device_id=sibling, device_id_type=MESH
        ).wait_recv()

    half = cols // 2
    plane = half * me_g
    from_x = half * (1 - me_g)

    def slab(d, c, start, count):
        owner = flip(hh, d) * 2 + c
        return wbuf.at[pl.ds(pl.multiple_of(owner * cols + start, half), count), :]

    if gather:
        own = w_hbm.at[pl.ds(pl.multiple_of(plane, half), half), :]
        for d in range(1, SPLIT):
            send(own, slab(0, cc, plane, half), wz_s.at[d], wz_r.at[d], zmate[d])
        send(w_hbm, slab(0, cc, 0, cols), wc_s.at[0, 0], wc_r.at[0, 0], sibling)

    lane_group = lax.broadcasted_iota(jnp.int32, (width, LANES), 1) * per_group
    channel = lax.broadcasted_iota(jnp.int32, (width, LANES), 0)
    member = ((channel >= lane_group) & (channel < lane_group + per_group)).astype(jnp.float32)

    member = member.astype(jnp.bfloat16)

    def thirds(line):
        high = line.astype(jnp.bfloat16).astype(jnp.float32)
        rest = line - high
        middle = rest.astype(jnp.bfloat16).astype(jnp.float32)
        return [high, middle, rest - middle]

    def stack(lines):
        wide = lines[0].shape[1]
        lines = lines + [jnp.zeros((16 - len(lines), wide), jnp.float32)]
        return jnp.concatenate(lines, axis=0).astype(jnp.bfloat16)

    def group_sum(line):
        sums = jnp.dot(stack(thirds(line)), member, preferred_element_type=jnp.float32)
        return sums[0:1] + sums[1:2] + sums[2:3]

    def spread(*lines):
        split = [part for line in lines for part in thirds(line)]
        wide = lax.dot_general(
            stack(split), member, (((1,), (1,)), ((), ())), preferred_element_type=jnp.float32
        )
        return [wide[i : i + 1] + wide[i + 1 : i + 2] + wide[i + 2 : i + 3] for i in range(0, len(split), 3)]

    load_control.wait()
    local_count = float(rows * per_group)
    control_f = control_ref[...].astype(jnp.float32)
    col_sum = jnp.sum(control_f, axis=0, keepdims=True)
    local_mean = group_sum(col_sum) / local_count
    off = control_f - spread(local_mean)[0]
    col_sq = jnp.sum(off * off, axis=0, keepdims=True)
    local_m2 = group_sum(col_sq)
    stat[0, 0] = jnp.broadcast_to(local_mean, (8, LANES))
    stat[0, 1] = jnp.broadcast_to(local_m2, (8, LANES))
    for f in range(1, span):
        send(stat.at[0], stat.at[f], stat_s.at[f], stat_r.at[f], peer[f])
    for f in range(1, span):
        arrive(stat.at[f], stat_s.at[f], stat_r.at[f])
    mean = stat[0, 0, 0:1]
    m2 = stat[0, 1, 0:1]
    for f in range(1, span):
        mean = mean + stat[f, 0, 0:1]
        m2 = m2 + stat[f, 1, 0:1]
    mean = mean / span
    for f in range(span):
        gap = stat[f, 0, 0:1] - mean
        m2 = m2 + local_count * (gap * gap)
    var = m2 / (local_count * span)
    inv = 1.0 / jnp.sqrt(var + 1e-05)
    mean_line, inv_line = spread(mean, inv)
    nbuf[0:rows, :] = ((control_ref[...].astype(jnp.float32) - mean_line) * inv_line).astype(jnp.bfloat16)
    if gather:
        send(nbuf.at[0:rows, :], nbuf.at[rows : 2 * rows, :], ny_s, ny_r, ymate[1])
    load_tokens.wait()

    if gather:
        half_block = width // 4

        def multiply(p):
            place = pl.ds(pl.multiple_of(p * half_block, half_block), half_block)
            residual = lax.dot_general(
                nbuf[...], wbuf[place, :], (((1,), (1,)), ((), ())), preferred_element_type=jnp.float32
            )
            mine[p] = residual[0:rows]
            theirs[p] = residual[rows : 2 * rows].astype(jnp.bfloat16)

        load_w.wait()
        for d in range(1, SPLIT):
            part = slab(d, cc, plane, half)
            arrive(part, wz_s.at[d], wz_r.at[d])
            send(part, part, wx_s.at[d], wx_r.at[d], xmate)
            send(part, part, wc_s.at[0, d], wc_r.at[0, d], sibling)
        for d in range(1, SPLIT):
            part = slab(d, cc, from_x, half)
            arrive(part, wx_s.at[d], wx_r.at[d])
            send(part, part, wc_s.at[1, d], wc_r.at[1, d], sibling)
        arrive(nbuf.at[rows : 2 * rows, :], ny_s, ny_r)
        arrive(slab(0, 1 - cc, 0, cols), wc_s.at[0, 0], wc_r.at[0, 0])
        for step in range(2):
            for d in range(2 * step, 2 * step + 2):
                if d > 0:
                    arrive(slab(d, 1 - cc, plane, half), wc_s.at[0, d], wc_r.at[0, d])
                    arrive(slab(d, 1 - cc, from_x, half), wc_s.at[1, d], wc_r.at[1, d])
            place = flip(hh // 2, step)
            multiply(place)
            send(theirs.at[place], rbuf.at[place], ry_s.at[step], ry_r.at[step], ymate[1])
        for step in range(2):
            place = flip(hh // 2, step)
            arrive(rbuf.at[place], ry_s.at[step], ry_r.at[step])
        for p in range(2):
            got = rbuf[p].astype(jnp.float32)
            low = jnp.where(uu == 0, mine[p], got)
            high = jnp.where(uu == 0, got, mine[p])
            cut = half_block // 2
            residual = jnp.concatenate([low[:, :cut], high[:, :cut], low[:, cut:], high[:, cut:]], axis=1)
            place = slice(2 * p * half_block, 2 * (p + 1) * half_block)
            hidden[:, place] = (tokens_ref[:, place].astype(jnp.float32) + residual).astype(jnp.bfloat16)
    else:
        load_w.wait()
        residual = lax.dot_general(
            nbuf[0:rows, :], wbuf[...], (((1,), (1,)), ((), ())), preferred_element_type=jnp.float32
        )
        hidden[...] = (tokens_ref[...].astype(jnp.float32) + residual).astype(jnp.bfloat16)

    hidden_f = hidden[...].astype(jnp.float32)
    tok_mean = jnp.mean(hidden_f, axis=-1, keepdims=True)
    tok_dev = hidden_f - tok_mean
    tok_var = jnp.mean(tok_dev * tok_dev, axis=-1, keepdims=True)
    layered = tok_dev / jnp.sqrt(tok_var + 1e-06)
    adapted[...] = (layered * (1.0 + mod_ref[1:2, :]) + mod_ref[0:1, :]).astype(jnp.bfloat16)

    features = HEADS * HEAD
    left = lax.broadcasted_iota(jnp.int32, (rows, LANES), 1) < HEAD
    load_qkv.wait()

    def project(at_col):
        return jnp.dot(
            adapted[...], qkv_w[:, at_col : at_col + features], preferred_element_type=jnp.float32
        )

    def tile(array, i):
        return array[:, i * LANES : (i + 1) * LANES]

    def lone(array, g):
        held = tile(array, SPLIT + g // 2)
        return held if g % 2 == 0 else pltpu.roll(held, HEAD, 1)

    def lone_right(array, g):
        held = tile(array, SPLIT + g // 2)
        return held if g % 2 == 1 else pltpu.roll(held, HEAD, 1)

    query = project(0) * (1.0 / HEAD**0.5)
    for g in range(SPLIT):
        qpack[g, :, 0:LANES] = tile(query, g).astype(jnp.bfloat16)
        qpack[g, :, LANES : 2 * LANES] = jnp.where(left, lone(query, g), 0.0).astype(jnp.bfloat16)
    def qpart(d):
        return qbuf.at[pl.ds(d * rows, rows), :]

    for d in range(1, SPLIT):
        send(qpack.at[flip(hh, d)], qpart(d), q_s.at[d], q_r.at[d], zmate[d])
    qbuf[0:rows, :] = qpack[hh]

    key = project(features)
    value = project(2 * features)
    for g in range(SPLIT):
        pack[g, :, 0:LANES] = tile(key, g).astype(jnp.bfloat16)
        pack[g, :, LANES : 2 * LANES] = jnp.where(left, lone(key, g), lone_right(value, g)).astype(jnp.bfloat16)
        pack[g, :, 2 * LANES : 3 * LANES] = tile(value, g).astype(jnp.bfloat16)

    def spot(e, d, par):
        first = ((e * SPLIT + d) * 2 + par) * rows
        return kvb.at[pl.ds(first, rows), :]

    for d in range(1, SPLIT):
        send(pack.at[flip(hh, d)], spot(0, d, 0), kz_s.at[d], kz_r.at[d], zmate[d])
    kvb[0:rows, :] = pack[hh]

    def relay_kv(d):
        for f in range(1, pairs):
            send(spot(0, d, 0), spot(pairs - f, d, 0), ky_s.at[f, d], ky_r.at[f, d], ymate[f])
        send(spot(0, d, 0), spot(0, d, 1), kc_s.at[0, d], kc_r.at[0, d], sibling)

    def take_z(d):
        arrive(spot(0, d, 0), kz_s.at[d], kz_r.at[d])
        relay_kv(d)

    def take_y(e, d):
        f = pairs - e
        arrive(spot(e, d, 0), ky_s.at[f, d], ky_r.at[f, d])
        send(spot(e, d, 0), spot(e, d, 1), kc_s.at[e, d], kc_r.at[e, d], sibling)

    def take_c(e, part):
        for d in (2 * part, 2 * part + 1):
            arrive(spot(e, d, 1), kc_s.at[e, d], kc_r.at[e, d])

    keys = SPLIT * rows
    deep = QUERY_TILE
    left_q = lax.broadcasted_iota(jnp.int32, (deep, LANES), 1) < HEAD

    def absorb(at_row, e, part):
        first = (2 * e + part) * keys
        mine_q = pl.ds(at_row, deep)
        for h in range(3):
            if h < 2:
                q = qbuf[mine_q, 0:LANES]
                q = jnp.where(left_q if h == 0 else ~left_q, q, jnp.zeros_like(q))
            else:
                q = qbuf[mine_q, LANES : 2 * LANES]
            kt, vt = (0, 2) if h < 2 else (1, 1)
            k = kvb[first : first + keys, kt * LANES : (kt + 1) * LANES]
            v = kvb[first : first + keys, vt * LANES : (vt + 1) * LANES]
            scores = lax.dot_general(q, k, (((1,), (1,)), ((), ())), preferred_element_type=jnp.float32)
            tiles = [scores[:, i : i + LANES] for i in range(0, keys, LANES)]
            top = functools.reduce(jnp.maximum, tiles)
            top = jnp.broadcast_to(jnp.max(top, axis=-1, keepdims=True), top.shape)
            fresh = (e, part) == (0, 0)
            if not fresh:
                best = m_ref[h, mine_q, :]
                top = jnp.maximum(best, top)
                shrink = jnp.exp(best - top)
            m_ref[h, mine_q, :] = top
            expo = [jnp.exp(x - top) for x in tiles]
            total = functools.reduce(jnp.add, expo)
            probs = jnp.concatenate([x.astype(jnp.bfloat16) for x in expo], axis=1)
            mixed = jnp.dot(probs, v, preferred_element_type=jnp.float32)
            if not fresh:
                total = total + l_ref[h, mine_q, :] * shrink
                mixed = mixed + acc_ref[h, mine_q, :] * shrink
            l_ref[h, mine_q, :] = total
            acc_ref[h, mine_q, :] = mixed

    def absorb_all(e, part):
        @pl.loop(0, SPLIT * rows // deep)
        def _(t):
            absorb(pl.multiple_of(t * deep, deep), e, part)

    relay_kv(0)
    for d in range(1, SPLIT):
        arrive(qpart(d), q_s.at[d], q_r.at[d])
    take_z(1)
    take_c(0, 0)
    absorb_all(0, 0)
    for e in range(1, pairs):
        take_y(e, 0)
        take_y(e, 1)
        take_c(e, 0)
        absorb_all(e, 0)
    take_z(2)
    take_z(3)
    take_c(0, 1)
    absorb_all(0, 1)
    for e in range(1, pairs):
        take_y(e, 2)
        take_y(e, 3)
    for e in range(1, pairs):
        take_c(e, 1)
        if e < pairs - 1:
            absorb_all(e, 1)

    for at_row in reversed(range(0, SPLIT * rows, deep)):
        if pairs > 1:
            absorb(at_row, pairs - 1, 1)
        for t in range(at_row // rows, (at_row + deep) // rows):
            q_rows = slice(t * rows, (t + 1) * rows)
            mixed = [
                acc_ref[h, q_rows, :] / jnp.sum(l_ref[h, q_rows, :], axis=-1, keepdims=True) for h in range(3)
            ]
            osend[t, :, 0:LANES] = jnp.where(left, mixed[0], mixed[1]).astype(jnp.bfloat16)
            osend[t, :, LANES : 2 * LANES] = mixed[2].astype(jnp.bfloat16)
            if t > 0:
                send(osend.at[t], obuf.at[hh], o_s.at[t], o_r.at[t], zmate[t])
    obuf[hh] = osend[0]
    for d in range(1, SPLIT):
        arrive(obuf.at[flip(hh, d)], o_s.at[d], o_r.at[d])
    load_out.wait()

    parts = [obuf[g, :, 0:LANES] for g in range(SPLIT)]
    for g in range(0, SPLIT, 2):
        first = pltpu.roll(obuf[g, :, LANES : 2 * LANES].astype(jnp.float32), HEAD, 1)
        second = obuf[g + 1, :, LANES : 2 * LANES].astype(jnp.float32)
        parts.append(jnp.where(left, first, second).astype(jnp.bfloat16))
    attended = jnp.concatenate(parts, axis=1)
    projected_out = jnp.dot(attended, out_w[...], preferred_element_type=jnp.float32)
    result_ref[...] = (hidden[...].astype(jnp.float32) + mod_ref[2:3, :] * projected_out).astype(jnp.bfloat16)

    for copy in sent:
        copy.wait_send()


def per_device(n, groups, tokens, control, zero_weight, modulation, qkv_weight, out_weight):
    rows, width = tokens.shape
    cols = zero_weight.shape[1]
    members = n // SPLIT
    pairs = members // 2
    span = n // VIEWS
    gather = groups == 2 and pairs == 2 and cols % 96 == 0
    weight = jnp.transpose(zero_weight)
    if not gather:
        weight = lax.all_gather(weight, "seq", axis=0, tiled=True)
    vmem = pl.BlockSpec(memory_space=pltpu.VMEM)
    anywhere = pl.BlockSpec(memory_space=pl.ANY)
    bf16, f32, dma = jnp.bfloat16, jnp.float32, pltpu.SemaphoreType.DMA
    features = HEADS * HEAD
    return pl.pallas_call(
        functools.partial(kernel, n, gather),
        out_shape=jax.ShapeDtypeStruct((rows, width), bf16),
        in_specs=[anywhere, anywhere, anywhere, vmem, anywhere, anywhere],
        out_specs=vmem,
        scratch_shapes=[
            pltpu.VMEM((rows, width), bf16),
            pltpu.VMEM((rows, width), bf16),
            pltpu.VMEM((width // 2 if gather else width, width), bf16),
            pltpu.VMEM((2 * rows, width), bf16),
            pltpu.VMEM((2, rows, width // 4), bf16),
            pltpu.VMEM((2, rows, width // 4), f32),
            pltpu.VMEM((2, rows, width // 4), bf16),
            pltpu.VMEM(qkv_weight.shape, bf16),
            pltpu.VMEM(out_weight.shape, bf16),
            pltpu.VMEM((span, 2, 8, LANES), f32),
            pltpu.VMEM((rows, width), bf16),
            pltpu.VMEM((rows, width), bf16),
            pltpu.VMEM((SPLIT, rows, 3 * LANES), bf16),
            pltpu.VMEM((SPLIT, rows, 2 * LANES), bf16),
            pltpu.VMEM((n * rows, 3 * LANES), bf16),
            pltpu.VMEM((SPLIT * rows, 2 * LANES), bf16),
            pltpu.VMEM((SPLIT, rows, 2 * LANES), bf16),
            pltpu.VMEM((SPLIT, rows, 2 * LANES), bf16),
            pltpu.VMEM((3, SPLIT * rows, LANES), f32),
            pltpu.VMEM((3, SPLIT * rows, LANES), f32),
            pltpu.VMEM((3, SPLIT * rows, LANES), f32),
            dma((5,)),
            dma((span,)),
            dma((span,)),
            dma((SPLIT,)),
            dma((SPLIT,)),
            dma(()),
            dma(()),
            dma((2,)),
            dma((2,)),
            dma((SPLIT,)),
            dma((SPLIT,)),
            dma((2, SPLIT)),
            dma((2, SPLIT)),
            dma((SPLIT,)),
            dma((SPLIT,)),
            dma((pairs, SPLIT)),
            dma((pairs, SPLIT)),
            dma((pairs, SPLIT)),
            dma((pairs, SPLIT)),
            dma((SPLIT,)),
            dma((SPLIT,)),
            dma((SPLIT,)),
            dma((SPLIT,)),
        ],
        compiler_params=pltpu.CompilerParams(
            collective_id=0, has_side_effects=True, vmem_limit_bytes=56 * 1024 * 1024
        ),
    )(tokens, control, weight, modulation, qkv_weight, out_weight)


def solution(mesh):
    placed = (
        P(("groups", "seq"), None),
        P(("groups", "seq"), None),
        P(None, "seq"),
        P("groups", None),
        P(),
        P(),
    )
    return jax.shard_map(
        functools.partial(per_device, mesh.shape["seq"], mesh.shape["groups"]),
        mesh=mesh,
        in_specs=placed,
        out_specs=P(("groups", "seq"), None),
        check_vma=False,
    )
```

```python
import functools

import jax
import jax.numpy as jnp
from jax import lax
from jax.experimental import pallas as pl
from jax.experimental.pallas import tpu as pltpu
from jax.sharding import PartitionSpec as P

HEADS = 12
HEAD = 64
GROUPS = 32
VIEWS = 8
EARLY_TILE = 512
LAST_TILE = 256
SPLIT = 4
LANES = 128
MESH = pl.DeviceIdType.MESH


def flip(index, d):
    if d == 0:
        return index
    if d == 1:
        return index + 1 - 2 * (index % 2)
    if d == 2:
        return index + 2 - 4 * (index // 2)
    return 3 - index


def kernel(
    n,
    gather,
    tokens_hbm,
    control_hbm,
    w_hbm,
    mod_ref,
    qkv_hbm,
    out_hbm,
    result_ref,
    tokens_ref,
    control_ref,
    wbuf,
    nbuf,
    rbuf,
    mine,
    theirs,
    qkv_w,
    out_w,
    stat,
    hidden,
    adapted,
    pack,
    qpack,
    kvb,
    qin,
    qbuf,
    obuf,
    osend,
    m_ref,
    l_ref,
    acc_ref,
    load_sem,
    stat_s,
    stat_r,
    wz_s,
    wz_r,
    ny_s,
    ny_r,
    ry_s,
    ry_r,
    wx_s,
    wx_r,
    wc_s,
    wc_r,
    kz_s,
    kz_r,
    ky_s,
    ky_r,
    kc_s,
    kc_r,
    q_s,
    q_r,
    o_s,
    o_r,
):
    rows, width = tokens_hbm.shape
    per_group = width // GROUPS
    cols = width // n
    members = n // SPLIT
    pairs = members // 2
    span = n // VIEWS
    me_g = lax.axis_index("groups")
    me = lax.axis_index("seq")
    hh = me // members
    uu = (me % members) // 2
    cc = me % 2

    def at(h, u, c):
        return (me_g, (h * pairs + u) * 2 + c)

    sibling = at(hh, uu, 1 - cc)
    zmate = [at(flip(hh, d), uu, cc) for d in range(SPLIT)]
    ymate = [at(hh, (uu + f) % pairs, cc) for f in range(pairs)]
    xmate = (1 - me_g, me)
    view_base = (me // span) * span
    peer = [(me_g, view_base + (me - view_base + f) % span) for f in range(span)]

    loads = [
        pltpu.make_async_copy(qkv_hbm, qkv_w, load_sem.at[0]),
        pltpu.make_async_copy(out_hbm, out_w, load_sem.at[1]),
        pltpu.make_async_copy(control_hbm, control_ref, load_sem.at[2]),
        pltpu.make_async_copy(tokens_hbm, tokens_ref, load_sem.at[3]),
    ]
    loads = [loads[2], loads[3], loads[0], loads[1]]
    load_control, load_tokens, load_qkv, load_out = loads
    if gather:
        place = pl.ds(pl.multiple_of((hh * 2 + cc) * cols, cols), cols)
        load_w = pltpu.make_async_copy(w_hbm, wbuf.at[place, :], load_sem.at[4])
    else:
        load_w = pltpu.make_async_copy(w_hbm, wbuf, load_sem.at[4])
    loads.append(load_w)
    for load in loads:
        load.start()

    barrier = pltpu.get_barrier_semaphore()
    greet = [sibling] + zmate[1:] + ymate[1:] + peer[1:] + ([xmate] if gather else [])
    for device in greet:
        pl.semaphore_signal(barrier, inc=1, device_id=device, device_id_type=MESH)

    pl.semaphore_wait(barrier, len(greet))

    sent = []

    def send(src, dst, ssem, rsem, device):
        copy = pltpu.make_async_remote_copy(
            src_ref=src, dst_ref=dst, send_sem=ssem, recv_sem=rsem, device_id=device, device_id_type=MESH
        )
        copy.start()
        sent.append(copy)

    def arrive(dst, ssem, rsem):
        pltpu.make_async_remote_copy(
            src_ref=dst, dst_ref=dst, send_sem=ssem, recv_sem=rsem, device_id=sibling, device_id_type=MESH
        ).wait_recv()

    half = cols // 2
    plane = half * me_g
    from_x = half * (1 - me_g)

    def slab(d, c, start, count):
        owner = flip(hh, d) * 2 + c
        return wbuf.at[pl.ds(pl.multiple_of(owner * cols + start, half), count), :]

    if gather:
        own = w_hbm.at[pl.ds(pl.multiple_of(plane, half), half), :]
        for d in range(1, SPLIT - 1):
            send(own, slab(0, cc, plane, half), wz_s.at[d], wz_r.at[d], zmate[d])
        send(w_hbm, slab(0, cc, 0, cols), wc_s.at[0, 0], wc_r.at[0, 0], sibling)

    lane_group = lax.broadcasted_iota(jnp.int32, (width, LANES), 1) * per_group
    channel = lax.broadcasted_iota(jnp.int32, (width, LANES), 0)
    member = ((channel >= lane_group) & (channel < lane_group + per_group)).astype(jnp.float32)

    member = member.astype(jnp.bfloat16)

    def thirds(line):
        high = line.astype(jnp.bfloat16).astype(jnp.float32)
        rest = line - high
        middle = rest.astype(jnp.bfloat16).astype(jnp.float32)
        return [high, middle, rest - middle]

    def stack(lines):
        wide = lines[0].shape[1]
        lines = lines + [jnp.zeros((16 - len(lines), wide), jnp.float32)]
        return jnp.concatenate(lines, axis=0).astype(jnp.bfloat16)

    def group_sum(line):
        sums = jnp.dot(stack(thirds(line)), member, preferred_element_type=jnp.float32)
        return sums[0:1] + sums[1:2] + sums[2:3]

    def spread(*lines):
        split = [part for line in lines for part in thirds(line)]
        wide = lax.dot_general(
            stack(split), member, (((1,), (1,)), ((), ())), preferred_element_type=jnp.float32
        )
        return [wide[i : i + 1] + wide[i + 1 : i + 2] + wide[i + 2 : i + 3] for i in range(0, len(split), 3)]

    load_control.wait()
    local_count = float(rows * per_group)
    control_f = control_ref[...].astype(jnp.float32)
    col_sum = jnp.sum(control_f, axis=0, keepdims=True)
    local_mean = group_sum(col_sum) / local_count
    off = control_f - spread(local_mean)[0]
    col_sq = jnp.sum(off * off, axis=0, keepdims=True)
    local_m2 = group_sum(col_sq)
    stat[0, 0] = jnp.broadcast_to(local_mean, (8, LANES))
    stat[0, 1] = jnp.broadcast_to(local_m2, (8, LANES))
    for f in range(1, span):
        send(stat.at[0], stat.at[f], stat_s.at[f], stat_r.at[f], peer[f])
    for f in range(1, span):
        arrive(stat.at[f], stat_s.at[f], stat_r.at[f])
    if gather:
        send(own, slab(0, cc, plane, half), wz_s.at[SPLIT - 1], wz_r.at[SPLIT - 1], zmate[SPLIT - 1])
    mean = stat[0, 0, 0:1]
    m2 = stat[0, 1, 0:1]
    for f in range(1, span):
        mean = mean + stat[f, 0, 0:1]
        m2 = m2 + stat[f, 1, 0:1]
    mean = mean / span
    for f in range(span):
        gap = stat[f, 0, 0:1] - mean
        m2 = m2 + local_count * (gap * gap)
    var = m2 / (local_count * span)
    inv = 1.0 / jnp.sqrt(var + 1e-05)
    mean_line, inv_line = spread(mean, inv)
    nbuf[0:rows, :] = ((control_ref[...].astype(jnp.float32) - mean_line) * inv_line).astype(jnp.bfloat16)
    if gather:
        send(nbuf.at[0:rows, :], nbuf.at[rows : 2 * rows, :], ny_s, ny_r, ymate[1])
    load_tokens.wait()

    if gather:
        half_block = width // 4

        def multiply(p):
            place = pl.ds(pl.multiple_of(p * half_block, half_block), half_block)
            residual = lax.dot_general(
                nbuf[...], wbuf[place, :], (((1,), (1,)), ((), ())), preferred_element_type=jnp.float32
            )
            mine[p] = residual[0:rows]
            theirs[p] = residual[rows : 2 * rows].astype(jnp.bfloat16)

        load_w.wait()
        for d in range(1, SPLIT):
            part = slab(d, cc, plane, half)
            arrive(part, wz_s.at[d], wz_r.at[d])
            send(part, part, wx_s.at[d], wx_r.at[d], xmate)
            send(part, part, wc_s.at[0, d], wc_r.at[0, d], sibling)
        for d in range(1, SPLIT):
            part = slab(d, cc, from_x, half)
            arrive(part, wx_s.at[d], wx_r.at[d])
            send(part, part, wc_s.at[1, d], wc_r.at[1, d], sibling)
        arrive(nbuf.at[rows : 2 * rows, :], ny_s, ny_r)
        arrive(slab(0, 1 - cc, 0, cols), wc_s.at[0, 0], wc_r.at[0, 0])
        for step in range(2):
            for d in range(2 * step, 2 * step + 2):
                if d > 0:
                    arrive(slab(d, 1 - cc, plane, half), wc_s.at[0, d], wc_r.at[0, d])
                    arrive(slab(d, 1 - cc, from_x, half), wc_s.at[1, d], wc_r.at[1, d])
            place = flip(hh // 2, step)
            multiply(place)
            send(theirs.at[place], rbuf.at[place], ry_s.at[step], ry_r.at[step], ymate[1])
        for step in range(2):
            place = flip(hh // 2, step)
            arrive(rbuf.at[place], ry_s.at[step], ry_r.at[step])
        for p in range(2):
            got = rbuf[p].astype(jnp.float32)
            low = jnp.where(uu == 0, mine[p], got)
            high = jnp.where(uu == 0, got, mine[p])
            cut = half_block // 2
            residual = jnp.concatenate([low[:, :cut], high[:, :cut], low[:, cut:], high[:, cut:]], axis=1)
            place = slice(2 * p * half_block, 2 * (p + 1) * half_block)
            hidden[:, place] = (tokens_ref[:, place].astype(jnp.float32) + residual).astype(jnp.bfloat16)
    else:
        load_w.wait()
        residual = lax.dot_general(
            nbuf[0:rows, :], wbuf[...], (((1,), (1,)), ((), ())), preferred_element_type=jnp.float32
        )
        hidden[...] = (tokens_ref[...].astype(jnp.float32) + residual).astype(jnp.bfloat16)

    hidden_f = hidden[...].astype(jnp.float32)
    tok_mean = jnp.mean(hidden_f, axis=-1, keepdims=True)
    tok_dev = hidden_f - tok_mean
    tok_var = jnp.mean(tok_dev * tok_dev, axis=-1, keepdims=True)
    layered = tok_dev / jnp.sqrt(tok_var + 1e-06)
    adapted[...] = (layered * (1.0 + mod_ref[1:2, :]) + mod_ref[0:1, :]).astype(jnp.bfloat16)

    features = HEADS * HEAD
    left = lax.broadcasted_iota(jnp.int32, (rows, LANES), 1) < HEAD
    load_qkv.wait()

    def project(at_col):
        return jnp.dot(
            adapted[...], qkv_w[:, at_col : at_col + features], preferred_element_type=jnp.float32
        )

    def tile(array, i):
        return array[:, i * LANES : (i + 1) * LANES]

    def lone(array, g):
        held = tile(array, SPLIT + g // 2)
        return held if g % 2 == 0 else pltpu.roll(held, HEAD, 1)

    def lone_right(array, g):
        held = tile(array, SPLIT + g // 2)
        return held if g % 2 == 1 else pltpu.roll(held, HEAD, 1)

    fold = rows // 2
    query = project(0) * (1.0 / HEAD**0.5)
    for g in range(SPLIT):
        qpack[g, 0:rows, :] = tile(query, g).astype(jnp.bfloat16)
        single = lone(query, g)
        qpack[g, rows : rows + fold, :] = jnp.where(
            left[:fold], single[:fold], pltpu.roll(single[fold:], HEAD, 1)
        ).astype(jnp.bfloat16)
    def qpart(d):
        return qin.at[d]

    def unfold_query(packed, d):
        qbuf[d * rows : (d + 1) * rows, 0:LANES] = packed[0:rows]
        single = packed[rows : rows + fold].astype(jnp.float32)
        single = jnp.concatenate([single, pltpu.roll(single, HEAD, 1)], axis=0)
        qbuf[d * rows : (d + 1) * rows, LANES : 2 * LANES] = jnp.where(left, single, 0.0).astype(jnp.bfloat16)

    for d in range(1, SPLIT):
        send(qpack.at[flip(hh, d)], qpart(d), q_s.at[d], q_r.at[d], zmate[d])
    unfold_query(qpack[hh], 0)

    key = project(features)
    value = project(2 * features)
    for g in range(SPLIT):
        pack[g, :, 0:LANES] = tile(key, g).astype(jnp.bfloat16)
        pack[g, :, LANES : 2 * LANES] = jnp.where(left, lone(key, g), lone_right(value, g)).astype(jnp.bfloat16)
        pack[g, :, 2 * LANES : 3 * LANES] = tile(value, g).astype(jnp.bfloat16)

    def spot(e, d, par):
        first = ((e * SPLIT + d) * 2 + par) * rows
        return kvb.at[pl.ds(first, rows), :]

    def send_kv(d):
        send(pack.at[flip(hh, d)], spot(0, d, 0), kz_s.at[d], kz_r.at[d], zmate[d])

    for d in range(1, SPLIT - 1):
        send_kv(d)
    kvb[0:rows, :] = pack[hh]

    def relay_kv(d):
        for f in range(1, pairs):
            send(spot(0, d, 0), spot(pairs - f, d, 0), ky_s.at[f, d], ky_r.at[f, d], ymate[f])
        send(spot(0, d, 0), spot(0, d, 1), kc_s.at[0, d], kc_r.at[0, d], sibling)

    def take_z(d):
        arrive(spot(0, d, 0), kz_s.at[d], kz_r.at[d])
        relay_kv(d)

    def take_y(e, d):
        f = pairs - e
        arrive(spot(e, d, 0), ky_s.at[f, d], ky_r.at[f, d])
        send(spot(e, d, 0), spot(e, d, 1), kc_s.at[e, d], kc_r.at[e, d], sibling)

    def take_c(e, part):
        for d in (2 * part, 2 * part + 1):
            arrive(spot(e, d, 1), kc_s.at[e, d], kc_r.at[e, d])

    keys = SPLIT * rows

    def absorb(at_row, deep, e, part):
        first = (2 * e + part) * keys
        mine_q = pl.ds(at_row, deep)
        left_q = lax.broadcasted_iota(jnp.int32, (deep, LANES), 1) < HEAD
        for h in range(3):
            if h < 2:
                q = qbuf[mine_q, 0:LANES]
                q = jnp.where(left_q if h == 0 else ~left_q, q, jnp.zeros_like(q))
            else:
                q = qbuf[mine_q, LANES : 2 * LANES]
            kt, vt = (0, 2) if h < 2 else (1, 1)
            k = kvb[first : first + keys, kt * LANES : (kt + 1) * LANES]
            v = kvb[first : first + keys, vt * LANES : (vt + 1) * LANES]
            scores = lax.dot_general(q, k, (((1,), (1,)), ((), ())), preferred_element_type=jnp.float32)
            tiles = [scores[:, i : i + LANES] for i in range(0, keys, LANES)]
            top = functools.reduce(jnp.maximum, tiles)
            top = jnp.broadcast_to(jnp.max(top, axis=-1, keepdims=True), top.shape)
            fresh = (e, part) == (0, 0)
            if not fresh:
                best = m_ref[h, mine_q, :]
                top = jnp.maximum(best, top)
                shrink = jnp.exp(best - top)
            m_ref[h, mine_q, :] = top
            expo = [jnp.exp(x - top) for x in tiles]
            total = functools.reduce(jnp.add, expo)
            probs = jnp.concatenate([x.astype(jnp.bfloat16) for x in expo], axis=1)
            mixed = jnp.dot(probs, v, preferred_element_type=jnp.float32)
            if not fresh:
                total = total + l_ref[h, mine_q, :] * shrink
                mixed = mixed + acc_ref[h, mine_q, :] * shrink
            l_ref[h, mine_q, :] = total
            acc_ref[h, mine_q, :] = mixed

    def absorb_all(e, part):
        @pl.loop(0, SPLIT * rows // EARLY_TILE)
        def _(t):
            absorb(pl.multiple_of(t * EARLY_TILE, EARLY_TILE), EARLY_TILE, e, part)

    relay_kv(0)
    for d in range(1, SPLIT):
        arrive(qpart(d), q_s.at[d], q_r.at[d])
        unfold_query(qin[d], d)
    take_z(1)
    send_kv(SPLIT - 1)
    take_c(0, 0)
    absorb_all(0, 0)
    for e in range(1, pairs):
        take_y(e, 0)
        take_y(e, 1)
        take_c(e, 0)
        absorb_all(e, 0)
    take_z(2)
    take_z(3)
    take_c(0, 1)
    absorb_all(0, 1)
    for e in range(1, pairs):
        take_y(e, 2)
        take_y(e, 3)
    for e in range(1, pairs):
        take_c(e, 1)
        if e < pairs - 1:
            absorb_all(e, 1)

    deep = LAST_TILE
    for at_row in reversed(range(0, SPLIT * rows, deep)):
        if pairs > 1:
            absorb(at_row, deep, pairs - 1, 1)
        for t in range(at_row // rows, (at_row + deep) // rows):
            q_rows = slice(t * rows, (t + 1) * rows)
            mixed = [
                acc_ref[h, q_rows, :] / jnp.sum(l_ref[h, q_rows, :], axis=-1, keepdims=True) for h in range(3)
            ]
            osend[t, 0:rows, :] = jnp.where(left, mixed[0], mixed[1]).astype(jnp.bfloat16)
            osend[t, rows : rows + fold, :] = jnp.where(
                left[:fold], pltpu.roll(mixed[2][:fold], HEAD, 1), mixed[2][fold:]
            ).astype(jnp.bfloat16)
            if t > 0:
                send(osend.at[t], obuf.at[hh], o_s.at[t], o_r.at[t], zmate[t])
    obuf[hh] = osend[0]
    for d in range(1, SPLIT):
        arrive(obuf.at[flip(hh, d)], o_s.at[d], o_r.at[d])
    load_out.wait()

    parts = [obuf[g, 0:rows, :] for g in range(SPLIT)]
    for g in range(0, SPLIT, 2):
        first = obuf[g, rows : rows + fold, :].astype(jnp.float32)
        second = obuf[g + 1, rows : rows + fold, :].astype(jnp.float32)
        upper = jnp.where(left[:fold], first, pltpu.roll(second, HEAD, 1))
        lower = jnp.where(left[:fold], pltpu.roll(first, HEAD, 1), second)
        parts.append(jnp.concatenate([upper, lower], axis=0).astype(jnp.bfloat16))
    attended = jnp.concatenate(parts, axis=1)
    projected_out = jnp.dot(attended, out_w[...], preferred_element_type=jnp.float32)
    result_ref[...] = (hidden[...].astype(jnp.float32) + mod_ref[2:3, :] * projected_out).astype(jnp.bfloat16)

    for copy in sent:
        copy.wait_send()


def per_device(n, groups, tokens, control, zero_weight, modulation, qkv_weight, out_weight):
    rows, width = tokens.shape
    cols = zero_weight.shape[1]
    members = n // SPLIT
    pairs = members // 2
    span = n // VIEWS
    gather = groups == 2 and pairs == 2 and cols % 96 == 0
    weight = jnp.transpose(zero_weight)
    if not gather:
        weight = lax.all_gather(weight, "seq", axis=0, tiled=True)
    vmem = pl.BlockSpec(memory_space=pltpu.VMEM)
    anywhere = pl.BlockSpec(memory_space=pl.ANY)
    bf16, f32, dma = jnp.bfloat16, jnp.float32, pltpu.SemaphoreType.DMA
    features = HEADS * HEAD
    return pl.pallas_call(
        functools.partial(kernel, n, gather),
        out_shape=jax.ShapeDtypeStruct((rows, width), bf16),
        in_specs=[anywhere, anywhere, anywhere, vmem, anywhere, anywhere],
        out_specs=vmem,
        scratch_shapes=[
            pltpu.VMEM((rows, width), bf16),
            pltpu.VMEM((rows, width), bf16),
            pltpu.VMEM((width // 2 if gather else width, width), bf16),
            pltpu.VMEM((2 * rows, width), bf16),
            pltpu.VMEM((2, rows, width // 4), bf16),
            pltpu.VMEM((2, rows, width // 4), f32),
            pltpu.VMEM((2, rows, width // 4), bf16),
            pltpu.VMEM(qkv_weight.shape, bf16),
            pltpu.VMEM(out_weight.shape, bf16),
            pltpu.VMEM((span, 2, 8, LANES), f32),
            pltpu.VMEM((rows, width), bf16),
            pltpu.VMEM((rows, width), bf16),
            pltpu.VMEM((SPLIT, rows, 3 * LANES), bf16),
            pltpu.VMEM((SPLIT, rows + rows // 2, LANES), bf16),
            pltpu.VMEM((n * rows, 3 * LANES), bf16),
            pltpu.VMEM((SPLIT, rows + rows // 2, LANES), bf16),
            pltpu.VMEM((SPLIT * rows, 2 * LANES), bf16),
            pltpu.VMEM((SPLIT, rows + rows // 2, LANES), bf16),
            pltpu.VMEM((SPLIT, rows + rows // 2, LANES), bf16),
            pltpu.VMEM((3, SPLIT * rows, LANES), f32),
            pltpu.VMEM((3, SPLIT * rows, LANES), f32),
            pltpu.VMEM((3, SPLIT * rows, LANES), f32),
            dma((5,)),
            dma((span,)),
            dma((span,)),
            dma((SPLIT,)),
            dma((SPLIT,)),
            dma(()),
            dma(()),
            dma((2,)),
            dma((2,)),
            dma((SPLIT,)),
            dma((SPLIT,)),
            dma((2, SPLIT)),
            dma((2, SPLIT)),
            dma((SPLIT,)),
            dma((SPLIT,)),
            dma((pairs, SPLIT)),
            dma((pairs, SPLIT)),
            dma((pairs, SPLIT)),
            dma((pairs, SPLIT)),
            dma((SPLIT,)),
            dma((SPLIT,)),
            dma((SPLIT,)),
            dma((SPLIT,)),
        ],
        compiler_params=pltpu.CompilerParams(
            collective_id=0, has_side_effects=True, vmem_limit_bytes=56 * 1024 * 1024
        ),
    )(tokens, control, weight, modulation, qkv_weight, out_weight)


def solution(mesh):
    placed = (
        P(("groups", "seq"), None),
        P(("groups", "seq"), None),
        P(None, "seq"),
        P("groups", None),
        P(),
        P(),
    )
    return jax.shard_map(
        functools.partial(per_device, mesh.shape["seq"], mesh.shape["groups"]),
        mesh=mesh,
        in_specs=placed,
        out_specs=P(("groups", "seq"), None),
        check_vma=False,
    )
```

```python
import functools

import jax
import jax.numpy as jnp
from jax import lax
from jax.experimental import pallas as pl
from jax.experimental.pallas import tpu as pltpu
from jax.sharding import PartitionSpec as P

HEADS = 12
HEAD = 64
GROUPS = 32
VIEWS = 8
EARLY_TILE = 512
LAST_TILE = 128
SPLIT = 4
LANES = 128
MESH = pl.DeviceIdType.MESH


def flip(index, d):
    if d == 0:
        return index
    if d == 1:
        return index + 1 - 2 * (index % 2)
    if d == 2:
        return index + 2 - 4 * (index // 2)
    return 3 - index


def kernel(
    n,
    gather,
    tokens_hbm,
    control_hbm,
    w_hbm,
    mod_ref,
    qkv_hbm,
    out_hbm,
    result_ref,
    tokens_ref,
    control_ref,
    wbuf,
    nbuf,
    rbuf,
    mine,
    theirs,
    qkv_w,
    out_w,
    stat,
    hidden,
    adapted,
    pack,
    qpack,
    kvb,
    qin,
    qbuf,
    obuf,
    osend,
    m_ref,
    l_ref,
    acc_ref,
    load_sem,
    stat_s,
    stat_r,
    wz_s,
    wz_r,
    ny_s,
    ny_r,
    ry_s,
    ry_r,
    wx_s,
    wx_r,
    wc_s,
    wc_r,
    kz_s,
    kz_r,
    ky_s,
    ky_r,
    kc_s,
    kc_r,
    q_s,
    q_r,
    o_s,
    o_r,
):
    rows, width = tokens_hbm.shape
    per_group = width // GROUPS
    cols = width // n
    members = n // SPLIT
    pairs = members // 2
    span = n // VIEWS
    me_g = lax.axis_index("groups")
    me = lax.axis_index("seq")
    hh = me // members
    uu = (me % members) // 2
    cc = me % 2

    def at(h, u, c):
        return (me_g, (h * pairs + u) * 2 + c)

    sibling = at(hh, uu, 1 - cc)
    zmate = [at(flip(hh, d), uu, cc) for d in range(SPLIT)]
    ymate = [at(hh, (uu + f) % pairs, cc) for f in range(pairs)]
    xmate = (1 - me_g, me)
    view_base = (me // span) * span
    peer = [(me_g, view_base + (me - view_base + f) % span) for f in range(span)]

    loads = [
        pltpu.make_async_copy(qkv_hbm, qkv_w, load_sem.at[0]),
        pltpu.make_async_copy(out_hbm, out_w, load_sem.at[1]),
        pltpu.make_async_copy(control_hbm, control_ref, load_sem.at[2]),
        pltpu.make_async_copy(tokens_hbm, tokens_ref, load_sem.at[3]),
    ]
    loads = [loads[2], loads[3], loads[0], loads[1]]
    load_control, load_tokens, load_qkv, load_out = loads
    if gather:
        place = pl.ds(pl.multiple_of((hh * 2 + cc) * cols, cols), cols)
        load_w = pltpu.make_async_copy(w_hbm, wbuf.at[place, :], load_sem.at[4])
    else:
        load_w = pltpu.make_async_copy(w_hbm, wbuf, load_sem.at[4])
    loads.append(load_w)
    for load in loads:
        load.start()

    barrier = pltpu.get_barrier_semaphore()
    greet = [sibling] + zmate[1:] + ymate[1:] + peer[1:] + ([xmate] if gather else [])
    for device in greet:
        pl.semaphore_signal(barrier, inc=1, device_id=device, device_id_type=MESH)

    pl.semaphore_wait(barrier, len(greet))

    sent = []

    def send(src, dst, ssem, rsem, device):
        copy = pltpu.make_async_remote_copy(
            src_ref=src, dst_ref=dst, send_sem=ssem, recv_sem=rsem, device_id=device, device_id_type=MESH
        )
        copy.start()
        sent.append(copy)

    def arrive(dst, ssem, rsem):
        pltpu.make_async_remote_copy(
            src_ref=dst, dst_ref=dst, send_sem=ssem, recv_sem=rsem, device_id=sibling, device_id_type=MESH
        ).wait_recv()

    half = cols // 2
    plane = half * me_g
    from_x = half * (1 - me_g)

    def slab(d, c, start, count):
        owner = flip(hh, d) * 2 + c
        return wbuf.at[pl.ds(pl.multiple_of(owner * cols + start, half), count), :]

    if gather:
        own = w_hbm.at[pl.ds(pl.multiple_of(plane, half), half), :]
        for d in range(1, SPLIT - 1):
            send(own, slab(0, cc, plane, half), wz_s.at[d], wz_r.at[d], zmate[d])
        send(w_hbm, slab(0, cc, 0, cols), wc_s.at[0, 0], wc_r.at[0, 0], sibling)

    lane_group = lax.broadcasted_iota(jnp.int32, (width, LANES), 1) * per_group
    channel = lax.broadcasted_iota(jnp.int32, (width, LANES), 0)
    member = ((channel >= lane_group) & (channel < lane_group + per_group)).astype(jnp.float32)

    member = member.astype(jnp.bfloat16)

    def thirds(line):
        high = line.astype(jnp.bfloat16).astype(jnp.float32)
        rest = line - high
        middle = rest.astype(jnp.bfloat16).astype(jnp.float32)
        return [high, middle, rest - middle]

    def stack(lines):
        wide = lines[0].shape[1]
        lines = lines + [jnp.zeros((16 - len(lines), wide), jnp.float32)]
        return jnp.concatenate(lines, axis=0).astype(jnp.bfloat16)

    def group_sum(line):
        sums = jnp.dot(stack(thirds(line)), member, preferred_element_type=jnp.float32)
        return sums[0:1] + sums[1:2] + sums[2:3]

    def spread(*lines):
        split = [part for line in lines for part in thirds(line)]
        wide = lax.dot_general(
            stack(split), member, (((1,), (1,)), ((), ())), preferred_element_type=jnp.float32
        )
        return [wide[i : i + 1] + wide[i + 1 : i + 2] + wide[i + 2 : i + 3] for i in range(0, len(split), 3)]

    load_control.wait()
    local_count = float(rows * per_group)
    control_f = control_ref[...].astype(jnp.float32)
    col_sum = jnp.sum(control_f, axis=0, keepdims=True)
    local_mean = group_sum(col_sum) / local_count
    off = control_f - spread(local_mean)[0]
    col_sq = jnp.sum(off * off, axis=0, keepdims=True)
    local_m2 = group_sum(col_sq)
    stat[0, 0] = jnp.broadcast_to(local_mean, (8, LANES))
    stat[0, 1] = jnp.broadcast_to(local_m2, (8, LANES))
    for f in range(1, span):
        send(stat.at[0], stat.at[f], stat_s.at[f], stat_r.at[f], peer[f])
    for f in range(1, span):
        arrive(stat.at[f], stat_s.at[f], stat_r.at[f])
    if gather:
        send(own, slab(0, cc, plane, half), wz_s.at[SPLIT - 1], wz_r.at[SPLIT - 1], zmate[SPLIT - 1])
    mean = stat[0, 0, 0:1]
    m2 = stat[0, 1, 0:1]
    for f in range(1, span):
        mean = mean + stat[f, 0, 0:1]
        m2 = m2 + stat[f, 1, 0:1]
    mean = mean / span
    for f in range(span):
        gap = stat[f, 0, 0:1] - mean
        m2 = m2 + local_count * (gap * gap)
    var = m2 / (local_count * span)
    inv = 1.0 / jnp.sqrt(var + 1e-05)
    mean_line, inv_line = spread(mean, inv)
    nbuf[0:rows, :] = ((control_ref[...].astype(jnp.float32) - mean_line) * inv_line).astype(jnp.bfloat16)
    if gather:
        send(nbuf.at[0:rows, :], nbuf.at[rows : 2 * rows, :], ny_s, ny_r, ymate[1])
    load_tokens.wait()

    if gather:
        half_block = width // 4

        def multiply(p):
            place = pl.ds(pl.multiple_of(p * half_block, half_block), half_block)
            residual = lax.dot_general(
                nbuf[...], wbuf[place, :], (((1,), (1,)), ((), ())), preferred_element_type=jnp.float32
            )
            mine[p] = residual[0:rows]
            theirs[p] = residual[rows : 2 * rows].astype(jnp.bfloat16)

        load_w.wait()
        for d in range(1, SPLIT):
            part = slab(d, cc, plane, half)
            arrive(part, wz_s.at[d], wz_r.at[d])
            send(part, part, wx_s.at[d], wx_r.at[d], xmate)
            send(part, part, wc_s.at[0, d], wc_r.at[0, d], sibling)
        def take_x(d):
            part = slab(d, cc, from_x, half)
            arrive(part, wx_s.at[d], wx_r.at[d])
            send(part, part, wc_s.at[1, d], wc_r.at[1, d], sibling)

        take_x(1)
        arrive(nbuf.at[rows : 2 * rows, :], ny_s, ny_r)
        arrive(slab(0, 1 - cc, 0, cols), wc_s.at[0, 0], wc_r.at[0, 0])
        for step in range(2):
            if step == 1:
                take_x(2)
                take_x(3)
            for d in range(2 * step, 2 * step + 2):
                if d > 0:
                    arrive(slab(d, 1 - cc, plane, half), wc_s.at[0, d], wc_r.at[0, d])
                    arrive(slab(d, 1 - cc, from_x, half), wc_s.at[1, d], wc_r.at[1, d])
            place = flip(hh // 2, step)
            multiply(place)
            send(theirs.at[place], rbuf.at[place], ry_s.at[step], ry_r.at[step], ymate[1])
        for step in range(2):
            p = flip(hh // 2, step)
            arrive(rbuf.at[p], ry_s.at[step], ry_r.at[step])
            got = rbuf[p].astype(jnp.float32)
            low = jnp.where(uu == 0, mine[p], got)
            high = jnp.where(uu == 0, got, mine[p])
            cut = half_block // 2
            residual = jnp.concatenate([low[:, :cut], high[:, :cut], low[:, cut:], high[:, cut:]], axis=1)
            place = pl.ds(pl.multiple_of(p * 2 * half_block, 2 * half_block), 2 * half_block)
            hidden[:, place] = (tokens_ref[:, place].astype(jnp.float32) + residual).astype(jnp.bfloat16)
    else:
        load_w.wait()
        residual = lax.dot_general(
            nbuf[0:rows, :], wbuf[...], (((1,), (1,)), ((), ())), preferred_element_type=jnp.float32
        )
        hidden[...] = (tokens_ref[...].astype(jnp.float32) + residual).astype(jnp.bfloat16)

    hidden_f = hidden[...].astype(jnp.float32)
    tok_mean = jnp.mean(hidden_f, axis=-1, keepdims=True)
    tok_dev = hidden_f - tok_mean
    tok_var = jnp.mean(tok_dev * tok_dev, axis=-1, keepdims=True)
    layered = tok_dev / jnp.sqrt(tok_var + 1e-06)
    adapted[...] = (layered * (1.0 + mod_ref[1:2, :]) + mod_ref[0:1, :]).astype(jnp.bfloat16)

    features = HEADS * HEAD
    left = lax.broadcasted_iota(jnp.int32, (rows, LANES), 1) < HEAD
    load_qkv.wait()

    def project(at_col):
        return jnp.dot(
            adapted[...], qkv_w[:, at_col : at_col + features], preferred_element_type=jnp.float32
        )

    def tile(array, i):
        return array[:, i * LANES : (i + 1) * LANES]

    def lone(array, g):
        held = tile(array, SPLIT + g // 2)
        return held if g % 2 == 0 else pltpu.roll(held, HEAD, 1)

    def lone_right(array, g):
        held = tile(array, SPLIT + g // 2)
        return held if g % 2 == 1 else pltpu.roll(held, HEAD, 1)

    fold = rows // 2
    query = project(0) * (1.0 / HEAD**0.5)
    for g in range(SPLIT):
        qpack[g, 0:rows, :] = tile(query, g).astype(jnp.bfloat16)
        single = lone(query, g)
        qpack[g, rows : rows + fold, :] = jnp.where(
            left[:fold], single[:fold], pltpu.roll(single[fold:], HEAD, 1)
        ).astype(jnp.bfloat16)
    def qpart(d):
        return qin.at[d]

    def unfold_query(packed, d):
        qbuf[d * rows : (d + 1) * rows, 0:LANES] = packed[0:rows]
        single = packed[rows : rows + fold].astype(jnp.float32)
        single = jnp.concatenate([single, pltpu.roll(single, HEAD, 1)], axis=0)
        qbuf[d * rows : (d + 1) * rows, LANES : 2 * LANES] = jnp.where(left, single, 0.0).astype(jnp.bfloat16)

    for d in range(1, SPLIT):
        send(qpack.at[flip(hh, d)], qpart(d), q_s.at[d], q_r.at[d], zmate[d])
    unfold_query(qpack[hh], 0)

    key = project(features)
    value = project(2 * features)
    for g in range(SPLIT):
        pack[g, :, 0:LANES] = tile(key, g).astype(jnp.bfloat16)
        pack[g, :, LANES : 2 * LANES] = jnp.where(left, lone(key, g), lone_right(value, g)).astype(jnp.bfloat16)
        pack[g, :, 2 * LANES : 3 * LANES] = tile(value, g).astype(jnp.bfloat16)

    def spot(e, d, par):
        first = ((e * SPLIT + d) * 2 + par) * rows
        return kvb.at[pl.ds(first, rows), :]

    def send_kv(d):
        send(pack.at[flip(hh, d)], spot(0, d, 0), kz_s.at[d], kz_r.at[d], zmate[d])

    for d in range(1, SPLIT - 1):
        send_kv(d)
    kvb[0:rows, :] = pack[hh]

    def relay_kv(d):
        for f in range(1, pairs):
            send(spot(0, d, 0), spot(pairs - f, d, 0), ky_s.at[f, d], ky_r.at[f, d], ymate[f])
        send(spot(0, d, 0), spot(0, d, 1), kc_s.at[0, d], kc_r.at[0, d], sibling)

    def take_z(d):
        arrive(spot(0, d, 0), kz_s.at[d], kz_r.at[d])
        relay_kv(d)

    def take_y(e, d):
        f = pairs - e
        arrive(spot(e, d, 0), ky_s.at[f, d], ky_r.at[f, d])
        send(spot(e, d, 0), spot(e, d, 1), kc_s.at[e, d], kc_r.at[e, d], sibling)

    def take_c(e, part):
        for d in (2 * part, 2 * part + 1):
            arrive(spot(e, d, 1), kc_s.at[e, d], kc_r.at[e, d])

    keys = SPLIT * rows

    def absorb(at_row, deep, e, part):
        first = (2 * e + part) * keys
        mine_q = pl.ds(at_row, deep)
        left_q = lax.broadcasted_iota(jnp.int32, (deep, LANES), 1) < HEAD
        for h in range(3):
            if h < 2:
                q = qbuf[mine_q, 0:LANES]
                q = jnp.where(left_q if h == 0 else ~left_q, q, jnp.zeros_like(q))
            else:
                q = qbuf[mine_q, LANES : 2 * LANES]
            kt, vt = (0, 2) if h < 2 else (1, 1)
            k = kvb[first : first + keys, kt * LANES : (kt + 1) * LANES]
            v = kvb[first : first + keys, vt * LANES : (vt + 1) * LANES]
            scores = lax.dot_general(q, k, (((1,), (1,)), ((), ())), preferred_element_type=jnp.float32)
            tiles = [scores[:, i : i + LANES] for i in range(0, keys, LANES)]
            top = functools.reduce(jnp.maximum, tiles)
            top = jnp.broadcast_to(jnp.max(top, axis=-1, keepdims=True), top.shape)
            fresh = (e, part) == (0, 0)
            if not fresh:
                best = m_ref[h, mine_q, :]
                top = jnp.maximum(best, top)
                shrink = jnp.exp(best - top)
            m_ref[h, mine_q, :] = top
            expo = [jnp.exp(x - top) for x in tiles]
            total = functools.reduce(jnp.add, expo)
            probs = jnp.concatenate([x.astype(jnp.bfloat16) for x in expo], axis=1)
            mixed = jnp.dot(probs, v, preferred_element_type=jnp.float32)
            if not fresh:
                total = total + l_ref[h, mine_q, :] * shrink
                mixed = mixed + acc_ref[h, mine_q, :] * shrink
            l_ref[h, mine_q, :] = total
            acc_ref[h, mine_q, :] = mixed

    def absorb_all(e, part):
        @pl.loop(0, SPLIT * rows // EARLY_TILE)
        def _(t):
            absorb(pl.multiple_of(t * EARLY_TILE, EARLY_TILE), EARLY_TILE, e, part)

    relay_kv(0)
    for d in range(1, SPLIT):
        arrive(qpart(d), q_s.at[d], q_r.at[d])
        unfold_query(qin[d], d)
    take_z(1)
    send_kv(SPLIT - 1)
    take_c(0, 0)
    absorb_all(0, 0)
    for e in range(1, pairs):
        take_y(e, 0)
        take_y(e, 1)
    take_z(2)
    for e in range(1, pairs):
        take_c(e, 0)
        absorb_all(e, 0)
    take_z(3)
    for e in range(1, pairs):
        take_y(e, 2)
    take_c(0, 1)
    absorb_all(0, 1)
    for e in range(1, pairs):
        take_y(e, 3)
    for e in range(1, pairs):
        take_c(e, 1)
        if e < pairs - 1:
            absorb_all(e, 1)

    deep = LAST_TILE
    for at_row in reversed(range(0, SPLIT * rows, deep)):
        if pairs > 1:
            absorb(at_row, deep, pairs - 1, 1)
        for t in range(at_row // rows, (at_row + deep) // rows):
            q_rows = slice(t * rows, (t + 1) * rows)
            mixed = [
                acc_ref[h, q_rows, :] / jnp.sum(l_ref[h, q_rows, :], axis=-1, keepdims=True) for h in range(3)
            ]
            osend[t, 0:rows, :] = jnp.where(left, mixed[0], mixed[1]).astype(jnp.bfloat16)
            osend[t, rows : rows + fold, :] = jnp.where(
                left[:fold], pltpu.roll(mixed[2][:fold], HEAD, 1), mixed[2][fold:]
            ).astype(jnp.bfloat16)
            if t > 0:
                send(osend.at[t], obuf.at[hh], o_s.at[t], o_r.at[t], zmate[t])
    obuf[hh] = osend[0]
    load_out.wait()

    def pair_product(owner):
        weights = out_w[pl.ds(pl.multiple_of(owner * LANES, LANES), LANES), :]
        return jnp.dot(obuf[owner, 0:rows, :], weights, preferred_element_type=jnp.float32)

    projected_out = pair_product(hh)
    for d in range(1, SPLIT):
        arrive(obuf.at[flip(hh, d)], o_s.at[d], o_r.at[d])
        projected_out = projected_out + pair_product(flip(hh, d))
    parts = []
    for g in range(0, SPLIT, 2):
        first = obuf[g, rows : rows + fold, :].astype(jnp.float32)
        second = obuf[g + 1, rows : rows + fold, :].astype(jnp.float32)
        upper = jnp.where(left[:fold], first, pltpu.roll(second, HEAD, 1))
        lower = jnp.where(left[:fold], pltpu.roll(first, HEAD, 1), second)
        parts.append(jnp.concatenate([upper, lower], axis=0).astype(jnp.bfloat16))
    singles = jnp.concatenate(parts, axis=1)
    projected_out = projected_out + jnp.dot(
        singles, out_w[SPLIT * LANES :, :], preferred_element_type=jnp.float32
    )
    result_ref[...] = (hidden[...].astype(jnp.float32) + mod_ref[2:3, :] * projected_out).astype(jnp.bfloat16)

    for copy in sent:
        copy.wait_send()


def per_device(n, groups, tokens, control, zero_weight, modulation, qkv_weight, out_weight):
    rows, width = tokens.shape
    cols = zero_weight.shape[1]
    members = n // SPLIT
    pairs = members // 2
    span = n // VIEWS
    gather = groups == 2 and pairs == 2 and cols % 96 == 0
    weight = jnp.transpose(zero_weight)
    if not gather:
        weight = lax.all_gather(weight, "seq", axis=0, tiled=True)
    vmem = pl.BlockSpec(memory_space=pltpu.VMEM)
    anywhere = pl.BlockSpec(memory_space=pl.ANY)
    bf16, f32, dma = jnp.bfloat16, jnp.float32, pltpu.SemaphoreType.DMA
    features = HEADS * HEAD
    return pl.pallas_call(
        functools.partial(kernel, n, gather),
        out_shape=jax.ShapeDtypeStruct((rows, width), bf16),
        in_specs=[anywhere, anywhere, anywhere, vmem, anywhere, anywhere],
        out_specs=vmem,
        scratch_shapes=[
            pltpu.VMEM((rows, width), bf16),
            pltpu.VMEM((rows, width), bf16),
            pltpu.VMEM((width // 2 if gather else width, width), bf16),
            pltpu.VMEM((2 * rows, width), bf16),
            pltpu.VMEM((2, rows, width // 4), bf16),
            pltpu.VMEM((2, rows, width // 4), f32),
            pltpu.VMEM((2, rows, width // 4), bf16),
            pltpu.VMEM(qkv_weight.shape, bf16),
            pltpu.VMEM(out_weight.shape, bf16),
            pltpu.VMEM((span, 2, 8, LANES), f32),
            pltpu.VMEM((rows, width), bf16),
            pltpu.VMEM((rows, width), bf16),
            pltpu.VMEM((SPLIT, rows, 3 * LANES), bf16),
            pltpu.VMEM((SPLIT, rows + rows // 2, LANES), bf16),
            pltpu.VMEM((n * rows, 3 * LANES), bf16),
            pltpu.VMEM((SPLIT, rows + rows // 2, LANES), bf16),
            pltpu.VMEM((SPLIT * rows, 2 * LANES), bf16),
            pltpu.VMEM((SPLIT, rows + rows // 2, LANES), bf16),
            pltpu.VMEM((SPLIT, rows + rows // 2, LANES), bf16),
            pltpu.VMEM((3, SPLIT * rows, LANES), f32),
            pltpu.VMEM((3, SPLIT * rows, LANES), f32),
            pltpu.VMEM((3, SPLIT * rows, LANES), f32),
            dma((5,)),
            dma((span,)),
            dma((span,)),
            dma((SPLIT,)),
            dma((SPLIT,)),
            dma(()),
            dma(()),
            dma((2,)),
            dma((2,)),
            dma((SPLIT,)),
            dma((SPLIT,)),
            dma((2, SPLIT)),
            dma((2, SPLIT)),
            dma((SPLIT,)),
            dma((SPLIT,)),
            dma((pairs, SPLIT)),
            dma((pairs, SPLIT)),
            dma((pairs, SPLIT)),
            dma((pairs, SPLIT)),
            dma((SPLIT,)),
            dma((SPLIT,)),
            dma((SPLIT,)),
            dma((SPLIT,)),
        ],
        compiler_params=pltpu.CompilerParams(
            collective_id=0, has_side_effects=True, vmem_limit_bytes=56 * 1024 * 1024
        ),
    )(tokens, control, weight, modulation, qkv_weight, out_weight)


def solution(mesh):
    placed = (
        P(("groups", "seq"), None),
        P(("groups", "seq"), None),
        P(None, "seq"),
        P("groups", None),
        P(),
        P(),
    )
    return jax.shard_map(
        functools.partial(per_device, mesh.shape["seq"], mesh.shape["groups"]),
        mesh=mesh,
        in_specs=placed,
        out_specs=P(("groups", "seq"), None),
        check_vma=False,
    )
```

```python
import functools

import jax
import jax.numpy as jnp
from jax import lax
from jax.experimental import pallas as pl
from jax.experimental.pallas import tpu as pltpu
from jax.sharding import PartitionSpec as P

HEADS = 12
HEAD = 64
GROUPS = 32
VIEWS = 8
EARLY_TILE = 256
LAST_TILE = 128
SPLIT = 4
LANES = 128
MESH = pl.DeviceIdType.MESH


def flip(index, d):
    if d == 0:
        return index
    if d == 1:
        return index + 1 - 2 * (index % 2)
    if d == 2:
        return index + 2 - 4 * (index // 2)
    return 3 - index


def kernel(
    n,
    gather,
    tokens_hbm,
    control_hbm,
    w_hbm,
    mod_ref,
    qkv_hbm,
    out_hbm,
    result_ref,
    tokens_ref,
    control_ref,
    wbuf,
    nbuf,
    rbuf,
    mine,
    theirs,
    qkv_w,
    out_w,
    stat,
    hidden,
    adapted,
    pack,
    qpack,
    kvb,
    qin,
    qbuf,
    obuf,
    osend,
    m_ref,
    l_ref,
    acc_ref,
    load_sem,
    stat_s,
    stat_r,
    wz_s,
    wz_r,
    ny_s,
    ny_r,
    ry_s,
    ry_r,
    wx_s,
    wx_r,
    wc_s,
    wc_r,
    kz_s,
    kz_r,
    ky_s,
    ky_r,
    kc_s,
    kc_r,
    q_s,
    q_r,
    o_s,
    o_r,
):
    rows, width = tokens_hbm.shape
    per_group = width // GROUPS
    cols = width // n
    members = n // SPLIT
    pairs = members // 2
    span = n // VIEWS
    me_g = lax.axis_index("groups")
    me = lax.axis_index("seq")
    hh = me // members
    uu = (me % members) // 2
    cc = me % 2

    def at(h, u, c):
        return (me_g, (h * pairs + u) * 2 + c)

    sibling = at(hh, uu, 1 - cc)
    zmate = [at(flip(hh, d), uu, cc) for d in range(SPLIT)]
    ymate = [at(hh, (uu + f) % pairs, cc) for f in range(pairs)]
    xmate = (1 - me_g, me)
    view_base = (me // span) * span
    peer = [(me_g, view_base + (me - view_base + f) % span) for f in range(span)]

    loads = [
        pltpu.make_async_copy(qkv_hbm, qkv_w, load_sem.at[0]),
        pltpu.make_async_copy(out_hbm, out_w, load_sem.at[1]),
        pltpu.make_async_copy(control_hbm, control_ref, load_sem.at[2]),
        pltpu.make_async_copy(tokens_hbm, tokens_ref, load_sem.at[3]),
    ]
    loads = [loads[2], loads[3], loads[0], loads[1]]
    load_control, load_tokens, load_qkv, load_out = loads
    if gather:
        place = pl.ds(pl.multiple_of((hh * 2 + cc) * cols, cols), cols)
        load_w = pltpu.make_async_copy(w_hbm, wbuf.at[place, :], load_sem.at[4])
    else:
        load_w = pltpu.make_async_copy(w_hbm, wbuf, load_sem.at[4])
    loads.append(load_w)
    for load in loads:
        load.start()

    barrier = pltpu.get_barrier_semaphore()
    greet = [sibling] + zmate[1:] + ymate[1:] + peer[1:] + ([xmate] if gather else [])
    for device in greet:
        pl.semaphore_signal(barrier, inc=1, device_id=device, device_id_type=MESH)

    pl.semaphore_wait(barrier, len(greet))

    sent = []

    def send(src, dst, ssem, rsem, device):
        copy = pltpu.make_async_remote_copy(
            src_ref=src, dst_ref=dst, send_sem=ssem, recv_sem=rsem, device_id=device, device_id_type=MESH
        )
        copy.start()
        sent.append(copy)

    def arrive(dst, ssem, rsem):
        pltpu.make_async_remote_copy(
            src_ref=dst, dst_ref=dst, send_sem=ssem, recv_sem=rsem, device_id=sibling, device_id_type=MESH
        ).wait_recv()

    half = cols // 2
    plane = half * me_g
    from_x = half * (1 - me_g)

    def slab(d, c, start, count):
        owner = flip(hh, d) * 2 + c
        return wbuf.at[pl.ds(pl.multiple_of(owner * cols + start, half), count), :]

    if gather:
        own = w_hbm.at[pl.ds(pl.multiple_of(plane, half), half), :]
        for d in range(1, SPLIT - 1):
            send(own, slab(0, cc, plane, half), wz_s.at[d], wz_r.at[d], zmate[d])
        send(w_hbm, slab(0, cc, 0, cols), wc_s.at[0, 0], wc_r.at[0, 0], sibling)

    lane_group = lax.broadcasted_iota(jnp.int32, (width, LANES), 1) * per_group
    channel = lax.broadcasted_iota(jnp.int32, (width, LANES), 0)
    member = ((channel >= lane_group) & (channel < lane_group + per_group)).astype(jnp.float32)

    member = member.astype(jnp.bfloat16)

    def thirds(line):
        high = line.astype(jnp.bfloat16).astype(jnp.float32)
        rest = line - high
        middle = rest.astype(jnp.bfloat16).astype(jnp.float32)
        return [high, middle, rest - middle]

    def stack(lines):
        wide = lines[0].shape[1]
        lines = lines + [jnp.zeros((16 - len(lines), wide), jnp.float32)]
        return jnp.concatenate(lines, axis=0).astype(jnp.bfloat16)

    def group_sum(line):
        sums = jnp.dot(stack(thirds(line)), member, preferred_element_type=jnp.float32)
        return sums[0:1] + sums[1:2] + sums[2:3]

    def spread(*lines):
        split = [part for line in lines for part in thirds(line)]
        wide = lax.dot_general(
            stack(split), member, (((1,), (1,)), ((), ())), preferred_element_type=jnp.float32
        )
        return [wide[i : i + 1] + wide[i + 1 : i + 2] + wide[i + 2 : i + 3] for i in range(0, len(split), 3)]

    load_control.wait()
    local_count = float(rows * per_group)
    control_f = control_ref[...].astype(jnp.float32)
    col_sum = jnp.sum(control_f, axis=0, keepdims=True)
    local_mean = group_sum(col_sum) / local_count
    off = control_f - spread(local_mean)[0]
    col_sq = jnp.sum(off * off, axis=0, keepdims=True)
    local_m2 = group_sum(col_sq)
    stat[0, 0] = jnp.broadcast_to(local_mean, (8, LANES))
    stat[0, 1] = jnp.broadcast_to(local_m2, (8, LANES))
    for f in range(1, span):
        send(stat.at[0], stat.at[f], stat_s.at[f], stat_r.at[f], peer[f])
    for f in range(1, span):
        arrive(stat.at[f], stat_s.at[f], stat_r.at[f])
    if gather:
        send(own, slab(0, cc, plane, half), wz_s.at[SPLIT - 1], wz_r.at[SPLIT - 1], zmate[SPLIT - 1])
    mean = stat[0, 0, 0:1]
    m2 = stat[0, 1, 0:1]
    for f in range(1, span):
        mean = mean + stat[f, 0, 0:1]
        m2 = m2 + stat[f, 1, 0:1]
    mean = mean / span
    for f in range(span):
        gap = stat[f, 0, 0:1] - mean
        m2 = m2 + local_count * (gap * gap)
    var = m2 / (local_count * span)
    inv = 1.0 / jnp.sqrt(var + 1e-05)
    mean_line, inv_line = spread(mean, inv)
    nbuf[0:rows, :] = ((control_ref[...].astype(jnp.float32) - mean_line) * inv_line).astype(jnp.bfloat16)
    if gather:
        send(nbuf.at[0:rows, :], nbuf.at[rows : 2 * rows, :], ny_s, ny_r, ymate[1])
    load_tokens.wait()

    if gather:
        half_block = width // 4

        def multiply(p):
            place = pl.ds(pl.multiple_of(p * half_block, half_block), half_block)
            residual = lax.dot_general(
                nbuf[...], wbuf[place, :], (((1,), (1,)), ((), ())), preferred_element_type=jnp.float32
            )
            mine[p] = residual[0:rows]
            theirs[p] = residual[rows : 2 * rows].astype(jnp.bfloat16)

        load_w.wait()
        for d in range(1, SPLIT):
            part = slab(d, cc, plane, half)
            arrive(part, wz_s.at[d], wz_r.at[d])
            send(part, part, wx_s.at[d], wx_r.at[d], xmate)
            send(part, part, wc_s.at[0, d], wc_r.at[0, d], sibling)
        def take_x(d):
            part = slab(d, cc, from_x, half)
            arrive(part, wx_s.at[d], wx_r.at[d])
            send(part, part, wc_s.at[1, d], wc_r.at[1, d], sibling)

        take_x(1)
        arrive(nbuf.at[rows : 2 * rows, :], ny_s, ny_r)
        arrive(slab(0, 1 - cc, 0, cols), wc_s.at[0, 0], wc_r.at[0, 0])
        for step in range(2):
            if step == 1:
                take_x(2)
                take_x(3)
            for d in range(2 * step, 2 * step + 2):
                if d > 0:
                    arrive(slab(d, 1 - cc, plane, half), wc_s.at[0, d], wc_r.at[0, d])
                    arrive(slab(d, 1 - cc, from_x, half), wc_s.at[1, d], wc_r.at[1, d])
            place = flip(hh // 2, step)
            multiply(place)
            send(theirs.at[place], rbuf.at[place], ry_s.at[step], ry_r.at[step], ymate[1])
        for step in range(2):
            p = flip(hh // 2, step)
            arrive(rbuf.at[p], ry_s.at[step], ry_r.at[step])
            got = rbuf[p].astype(jnp.float32)
            low = jnp.where(uu == 0, mine[p], got)
            high = jnp.where(uu == 0, got, mine[p])
            cut = half_block // 2
            residual = jnp.concatenate([low[:, :cut], high[:, :cut], low[:, cut:], high[:, cut:]], axis=1)
            place = pl.ds(pl.multiple_of(p * 2 * half_block, 2 * half_block), 2 * half_block)
            hidden[:, place] = (tokens_ref[:, place].astype(jnp.float32) + residual).astype(jnp.bfloat16)
    else:
        load_w.wait()
        residual = lax.dot_general(
            nbuf[0:rows, :], wbuf[...], (((1,), (1,)), ((), ())), preferred_element_type=jnp.float32
        )
        hidden[...] = (tokens_ref[...].astype(jnp.float32) + residual).astype(jnp.bfloat16)

    hidden_f = hidden[...].astype(jnp.float32)
    tok_mean = jnp.mean(hidden_f, axis=-1, keepdims=True)
    tok_dev = hidden_f - tok_mean
    tok_var = jnp.mean(tok_dev * tok_dev, axis=-1, keepdims=True)
    layered = tok_dev / jnp.sqrt(tok_var + 1e-06)
    adapted[...] = (layered * (1.0 + mod_ref[1:2, :]) + mod_ref[0:1, :]).astype(jnp.bfloat16)

    features = HEADS * HEAD
    left = lax.broadcasted_iota(jnp.int32, (rows, LANES), 1) < HEAD
    load_qkv.wait()

    def project(at_col):
        return jnp.dot(
            adapted[...], qkv_w[:, at_col : at_col + features], preferred_element_type=jnp.float32
        )

    def tile(array, i):
        return array[:, i * LANES : (i + 1) * LANES]

    def lone(array, g):
        held = tile(array, SPLIT + g // 2)
        return held if g % 2 == 0 else pltpu.roll(held, HEAD, 1)

    def lone_right(array, g):
        held = tile(array, SPLIT + g // 2)
        return held if g % 2 == 1 else pltpu.roll(held, HEAD, 1)

    fold = rows // 2
    query = project(0) * (1.0 / HEAD**0.5)
    for g in range(SPLIT):
        qpack[g, 0:rows, :] = tile(query, g).astype(jnp.bfloat16)
        single = lone(query, g)
        qpack[g, rows : rows + fold, :] = jnp.where(
            left[:fold], single[:fold], pltpu.roll(single[fold:], HEAD, 1)
        ).astype(jnp.bfloat16)
    def qpart(d):
        return qin.at[d]

    def unfold_query(packed, d):
        qbuf[d * rows : (d + 1) * rows, 0:LANES] = packed[0:rows]
        single = packed[rows : rows + fold].astype(jnp.float32)
        single = jnp.concatenate([single, pltpu.roll(single, HEAD, 1)], axis=0)
        qbuf[d * rows : (d + 1) * rows, LANES : 2 * LANES] = jnp.where(left, single, 0.0).astype(jnp.bfloat16)

    def send_q(d):
        send(qpack.at[flip(hh, d)], qpart(d), q_s.at[d], q_r.at[d], zmate[d])

    def take_q(d):
        arrive(qpart(d), q_s.at[d], q_r.at[d])
        unfold_query(qin[d], d)

    send_q(1)
    unfold_query(qpack[hh], 0)

    key = project(features)
    value = project(2 * features)
    for g in range(SPLIT):
        pack[g, :, 0:LANES] = tile(key, g).astype(jnp.bfloat16)
        pack[g, :, LANES : 2 * LANES] = jnp.where(left, lone(key, g), lone_right(value, g)).astype(jnp.bfloat16)
        pack[g, :, 2 * LANES : 3 * LANES] = tile(value, g).astype(jnp.bfloat16)

    def spot(e, d, par):
        first = ((e * SPLIT + d) * 2 + par) * rows
        return kvb.at[pl.ds(first, rows), :]

    def send_kv(d):
        send(pack.at[flip(hh, d)], spot(0, d, 0), kz_s.at[d], kz_r.at[d], zmate[d])

    for d in range(1, SPLIT - 1):
        send_kv(d)
    kvb[0:rows, :] = pack[hh]

    def relay_kv(d):
        for f in range(1, pairs):
            send(spot(0, d, 0), spot(pairs - f, d, 0), ky_s.at[f, d], ky_r.at[f, d], ymate[f])
        send(spot(0, d, 0), spot(0, d, 1), kc_s.at[0, d], kc_r.at[0, d], sibling)

    def take_z(d):
        arrive(spot(0, d, 0), kz_s.at[d], kz_r.at[d])
        relay_kv(d)

    def take_y(e, d):
        f = pairs - e
        arrive(spot(e, d, 0), ky_s.at[f, d], ky_r.at[f, d])
        send(spot(e, d, 0), spot(e, d, 1), kc_s.at[e, d], kc_r.at[e, d], sibling)

    def take_c(e, part):
        for d in (2 * part, 2 * part + 1):
            arrive(spot(e, d, 1), kc_s.at[e, d], kc_r.at[e, d])

    keys = SPLIT * rows

    def absorb(at_row, deep, e, part):
        first = (2 * e + part) * keys
        mine_q = pl.ds(at_row, deep)
        left_q = lax.broadcasted_iota(jnp.int32, (deep, LANES), 1) < HEAD
        for h in range(3):
            if h < 2:
                q = qbuf[mine_q, 0:LANES]
                q = jnp.where(left_q if h == 0 else ~left_q, q, jnp.zeros_like(q))
            else:
                q = qbuf[mine_q, LANES : 2 * LANES]
            kt, vt = (0, 2) if h < 2 else (1, 1)
            k = kvb[first : first + keys, kt * LANES : (kt + 1) * LANES]
            v = kvb[first : first + keys, vt * LANES : (vt + 1) * LANES]
            scores = lax.dot_general(q, k, (((1,), (1,)), ((), ())), preferred_element_type=jnp.float32)
            tiles = [scores[:, i : i + LANES] for i in range(0, keys, LANES)]
            top = functools.reduce(jnp.maximum, tiles)
            top = jnp.broadcast_to(jnp.max(top, axis=-1, keepdims=True), top.shape)
            fresh = (e, part) == (0, 0)
            if not fresh:
                best = m_ref[h, mine_q, :]
                top = jnp.maximum(best, top)
                shrink = jnp.exp(best - top)
            m_ref[h, mine_q, :] = top
            expo = [jnp.exp(x - top) for x in tiles]
            total = functools.reduce(jnp.add, expo)
            probs = jnp.concatenate([x.astype(jnp.bfloat16) for x in expo], axis=1)
            mixed = jnp.dot(probs, v, preferred_element_type=jnp.float32)
            if not fresh:
                total = total + l_ref[h, mine_q, :] * shrink
                mixed = mixed + acc_ref[h, mine_q, :] * shrink
            l_ref[h, mine_q, :] = total
            acc_ref[h, mine_q, :] = mixed

    near, far = 0, EARLY_TILE

    relay_kv(0)
    take_q(1)
    take_z(1)
    send_kv(SPLIT - 1)
    send_q(2)
    send_q(3)
    take_c(0, 0)
    absorb(near, EARLY_TILE, 0, 0)
    for e in range(1, pairs):
        take_y(e, 0)
        take_y(e, 1)
    take_z(2)
    for e in range(1, pairs):
        take_c(e, 0)
        absorb(near, EARLY_TILE, e, 0)
    take_z(3)
    for e in range(1, pairs):
        take_y(e, 2)
    take_c(0, 1)
    absorb(near, EARLY_TILE, 0, 1)
    for e in range(1, pairs):
        take_y(e, 3)
    take_q(2)
    take_q(3)
    for e in range(pairs):
        absorb(far, EARLY_TILE, e, 0)
    absorb(far, EARLY_TILE, 0, 1)
    for e in range(1, pairs):
        take_c(e, 1)
        if e < pairs - 1:
            absorb(near, EARLY_TILE, e, 1)
            absorb(far, EARLY_TILE, e, 1)

    deep = LAST_TILE
    for at_row in reversed(range(0, SPLIT * rows, deep)):
        if pairs > 1:
            absorb(at_row, deep, pairs - 1, 1)
        for t in range(at_row // rows, (at_row + deep) // rows):
            q_rows = slice(t * rows, (t + 1) * rows)
            mixed = [
                acc_ref[h, q_rows, :] / jnp.sum(l_ref[h, q_rows, :], axis=-1, keepdims=True) for h in range(3)
            ]
            osend[t, 0:rows, :] = jnp.where(left, mixed[0], mixed[1]).astype(jnp.bfloat16)
            osend[t, rows : rows + fold, :] = jnp.where(
                left[:fold], pltpu.roll(mixed[2][:fold], HEAD, 1), mixed[2][fold:]
            ).astype(jnp.bfloat16)
            if t > 0:
                send(osend.at[t], obuf.at[hh], o_s.at[t], o_r.at[t], zmate[t])
    obuf[hh] = osend[0]
    load_out.wait()

    def pair_product(owner):
        weights = out_w[pl.ds(pl.multiple_of(owner * LANES, LANES), LANES), :]
        return jnp.dot(obuf[owner, 0:rows, :], weights, preferred_element_type=jnp.float32)

    projected_out = pair_product(hh)
    for d in range(1, SPLIT):
        arrive(obuf.at[flip(hh, d)], o_s.at[d], o_r.at[d])
        projected_out = projected_out + pair_product(flip(hh, d))
    parts = []
    for g in range(0, SPLIT, 2):
        first = obuf[g, rows : rows + fold, :].astype(jnp.float32)
        second = obuf[g + 1, rows : rows + fold, :].astype(jnp.float32)
        upper = jnp.where(left[:fold], first, pltpu.roll(second, HEAD, 1))
        lower = jnp.where(left[:fold], pltpu.roll(first, HEAD, 1), second)
        parts.append(jnp.concatenate([upper, lower], axis=0).astype(jnp.bfloat16))
    singles = jnp.concatenate(parts, axis=1)
    projected_out = projected_out + jnp.dot(
        singles, out_w[SPLIT * LANES :, :], preferred_element_type=jnp.float32
    )
    result_ref[...] = (hidden[...].astype(jnp.float32) + mod_ref[2:3, :] * projected_out).astype(jnp.bfloat16)

    for copy in sent:
        copy.wait_send()


def per_device(n, groups, tokens, control, zero_weight, modulation, qkv_weight, out_weight):
    rows, width = tokens.shape
    cols = zero_weight.shape[1]
    members = n // SPLIT
    pairs = members // 2
    span = n // VIEWS
    gather = groups == 2 and pairs == 2 and cols % 96 == 0
    weight = jnp.transpose(zero_weight)
    if not gather:
        weight = lax.all_gather(weight, "seq", axis=0, tiled=True)
    vmem = pl.BlockSpec(memory_space=pltpu.VMEM)
    anywhere = pl.BlockSpec(memory_space=pl.ANY)
    bf16, f32, dma = jnp.bfloat16, jnp.float32, pltpu.SemaphoreType.DMA
    features = HEADS * HEAD
    return pl.pallas_call(
        functools.partial(kernel, n, gather),
        out_shape=jax.ShapeDtypeStruct((rows, width), bf16),
        in_specs=[anywhere, anywhere, anywhere, vmem, anywhere, anywhere],
        out_specs=vmem,
        scratch_shapes=[
            pltpu.VMEM((rows, width), bf16),
            pltpu.VMEM((rows, width), bf16),
            pltpu.VMEM((width // 2 if gather else width, width), bf16),
            pltpu.VMEM((2 * rows, width), bf16),
            pltpu.VMEM((2, rows, width // 4), bf16),
            pltpu.VMEM((2, rows, width // 4), f32),
            pltpu.VMEM((2, rows, width // 4), bf16),
            pltpu.VMEM(qkv_weight.shape, bf16),
            pltpu.VMEM(out_weight.shape, bf16),
            pltpu.VMEM((span, 2, 8, LANES), f32),
            pltpu.VMEM((rows, width), bf16),
            pltpu.VMEM((rows, width), bf16),
            pltpu.VMEM((SPLIT, rows, 3 * LANES), bf16),
            pltpu.VMEM((SPLIT, rows + rows // 2, LANES), bf16),
            pltpu.VMEM((n * rows, 3 * LANES), bf16),
            pltpu.VMEM((SPLIT, rows + rows // 2, LANES), bf16),
            pltpu.VMEM((SPLIT * rows, 2 * LANES), bf16),
            pltpu.VMEM((SPLIT, rows + rows // 2, LANES), bf16),
            pltpu.VMEM((SPLIT, rows + rows // 2, LANES), bf16),
            pltpu.VMEM((3, SPLIT * rows, LANES), f32),
            pltpu.VMEM((3, SPLIT * rows, LANES), f32),
            pltpu.VMEM((3, SPLIT * rows, LANES), f32),
            dma((5,)),
            dma((span,)),
            dma((span,)),
            dma((SPLIT,)),
            dma((SPLIT,)),
            dma(()),
            dma(()),
            dma((2,)),
            dma((2,)),
            dma((SPLIT,)),
            dma((SPLIT,)),
            dma((2, SPLIT)),
            dma((2, SPLIT)),
            dma((SPLIT,)),
            dma((SPLIT,)),
            dma((pairs, SPLIT)),
            dma((pairs, SPLIT)),
            dma((pairs, SPLIT)),
            dma((pairs, SPLIT)),
            dma((SPLIT,)),
            dma((SPLIT,)),
            dma((SPLIT,)),
            dma((SPLIT,)),
        ],
        compiler_params=pltpu.CompilerParams(
            collective_id=0, has_side_effects=True, vmem_limit_bytes=56 * 1024 * 1024
        ),
    )(tokens, control, weight, modulation, qkv_weight, out_weight)


def solution(mesh):
    placed = (
        P(("groups", "seq"), None),
        P(("groups", "seq"), None),
        P(None, "seq"),
        P("groups", None),
        P(),
        P(),
    )
    return jax.shard_map(
        functools.partial(per_device, mesh.shape["seq"], mesh.shape["groups"]),
        mesh=mesh,
        in_specs=placed,
        out_specs=P(("groups", "seq"), None),
        check_vma=False,
    )
```
